512 devices in a mesh: kring: 16 (over y_hi, x, core), orb: 32 (over y_lo, z).
Axes of the slice: x: 4, y: 4 (y_hi: 2, y_lo: 2; y = y_hi * 2 + y_lo), z: 16, core: 2. Of those that a mesh axis runs over, the one named last changes fastest.
Arguments:
- tau_slabs: bfloat16 [32, 2, 112, 28672], P('kring', None, None, 'orb'), may hold values from -0.005859375 to 0.005859375
- lambda_slabs: bfloat16 [32, 2, 112, 28672], P('kring', None, None, 'orb'), may hold values from -0.5 to 0.5
- aux_factor: bfloat16 [2, 2, 112, 53760], P(None, None, None, 'orb'), may hold values from -0.375 to 0.375
- transfer_table: int32 [32, 32], replicated, may hold values from 0 to 2, as said below
Outputs:
- gamma_density: float32 [2, 2, 112, 53760], P(None, None, 'kring', 'orb')
The draws below stay inside these ranges and needn't reach their ends.
Inputs may be any that keep to these rules, and one draw needn't show every extreme that they name: transfer_table[t, u] is the momentum transfer that Tau triple t and Lambda triple u contribute to, or 2 where they share no occupied k-pair; each Tau triple has one or two Lambda partners.
All inputs are finite; a program needn't handle non-finite values.
Results may differ from the reference program's by a relative error of at most 0.0029.
Values may be sent and summed in bfloat16 or wider, within the bound.
No kernel may reach another device: no remote copies, remote signals or barrier semaphores. Data moves between devices by JAX's collectives and lax.ppermute only.
A program may use at most 64 MiB of HBM per device.

```python
import jax
import jax.numpy as jnp
from jax import lax

V = 112
AUX = 480
NQ = 2
TRIP_DEV = 2
PAIRS = 256
KT = 32


def draw_transfer_table(key, part):
    key = jax.random.fold_in(key, 11)
    keys = jax.random.split(key, 5)
    groups = KT // TRIP_DEV
    triple_ids = jnp.arange(KT, dtype=jnp.int32)
    device_ids = triple_ids // TRIP_DEV
    offsets = jax.random.permutation(keys[0], groups).astype(jnp.int32)
    partner_device = (device_ids + offsets[device_ids]) % groups
    partner_local = jax.random.randint(keys[1], (KT,), 0, TRIP_DEV, dtype=jnp.int32)
    first_partner = partner_device * TRIP_DEV + partner_local
    second_partner = jax.random.permutation(keys[2], KT).astype(jnp.int32)
    first_value = (triple_ids + jax.random.randint(keys[3], (KT,), 0, 2, dtype=jnp.int32)) % NQ
    second_value = jax.random.randint(keys[4], (KT,), 0, NQ, dtype=jnp.int32)
    table = jnp.full((KT, KT), NQ, dtype=jnp.int32)
    table = table.at[triple_ids, second_partner].set(second_value)
    table = table.at[triple_ids, first_partner].set(first_value)
    return table


def levels(rng, dims, cuts, low, high):
    def one(axis_at, shards_of):
        draws = jax.random.uniform(jax.random.fold_in(jax.random.fold_in(rng, 6), axis_at), (shards_of,), jnp.float32, low / len(cuts), high / len(cuts))
        return jnp.repeat(jnp.exp(draws), dims[axis_at] // shards_of).reshape((-1,) + (1,) * (len(dims) - axis_at - 1))

    level = one(*cuts[0])
    for cut in cuts[1:]:
        level = level * one(*cut)
    return level


def bell_draw(rng, extent, width, most, pieces=(), kind=jnp.bfloat16):
    drawn = width * jax.random.normal(rng, extent, jnp.float32)
    if pieces:
        drawn = drawn * levels(rng, extent, pieces, -0.22, 0.18)
    return jnp.clip(drawn, -most, most).astype(kind)


def setup_inputs(seed: int = 0) -> dict:
    splits = jax.random.split(jax.random.key(seed), 5)
    return {
        "tau_slabs": bell_draw(splits[0], (KT, 2, V, PAIRS * V), (KT * PAIRS * V) ** -0.5, 0.005859375, ((0, 16), (3, 32))),
        "lambda_slabs": bell_draw(splits[1], (KT, 2, V, PAIRS * V), V ** -0.5, 0.5, ((0, 16), (3, 32))),
        "aux_factor": bell_draw(splits[2], (NQ, 2, V, AUX * V), (2 * V) ** -0.5, 0.375, ((3, 32),)),
        "transfer_table": draw_transfer_table(jax.random.fold_in(splits[4], 71), 0),
    }


def reference(tau_slabs, lambda_slabs, aux_factor, transfer_table):
    tau_rows = tau_slabs.reshape(KT * 2 * V, PAIRS * V)
    lambda_rows = lambda_slabs.reshape(KT * 2 * V, PAIRS * V)
    products = lax.dot_general(tau_rows, lambda_rows, (((1,), (1,)), ((), ())), preferred_element_type=jnp.float32)
    products = products.reshape(KT, 2, V, KT, 2, V)
    real_part = products[:, 0, :, :, 0, :] + products[:, 1, :, :, 1, :]
    imag_part = products[:, 1, :, :, 0, :] - products[:, 0, :, :, 1, :]
    stacked = jnp.stack([real_part, imag_part], 0)
    weights = (transfer_table[None] == jnp.arange(NQ, dtype=jnp.int32)[:, None, None]).astype(jnp.float32)
    density = jnp.einsum("qtu,rtaud->qrad", weights, stacked, precision=lax.Precision.HIGHEST).astype(jnp.bfloat16)
    upper = jnp.concatenate([density[:, 0], -density[:, 1]], 2)
    lower = jnp.concatenate([density[:, 1], density[:, 0]], 2)
    blocked = jnp.concatenate([upper, lower], 1).astype(jnp.float32)
    factors = aux_factor.reshape(NQ, 2 * V, AUX * V).astype(jnp.float32)
    gamma_block = jnp.einsum("qrd,qdc->qrc", blocked, factors, precision=lax.Precision.HIGHEST)
    return gamma_block.reshape(NQ, 2, V, AUX * V)
```

```python
import jax
import jax.numpy as jnp
from jax import lax
from jax.experimental import pallas as pl
from jax.experimental.pallas import tpu as pltpu
from jax.sharding import PartitionSpec as P

LANES = 128
SUBLANES = 8


def partner_slots(table, shape):
    none = 2
    column = lax.broadcasted_iota(jnp.int32, table.shape, 1)
    used = table != none
    first = jnp.min(jnp.where(used, column, table.shape[1] - 1), 1, keepdims=True)
    last = jnp.max(jnp.where(used, column, 0), 1, keepdims=True)
    first_q = jnp.sum(jnp.where(column == first, table, 0), 1, keepdims=True)
    last_q = jnp.sum(jnp.where(column == last, table, 0), 1, keepdims=True)
    last_q = jnp.where(last == first, none, last_q)
    place = lax.broadcasted_iota(jnp.int32, shape, 1)
    return jnp.where(
        place == 0, first, jnp.where(place == 1, last, jnp.where(place == 2, first_q, last_q))
    )


def pack_kernel(
    tau_ref, lambda_ref, table_ref, packed_ref, slots_ref, both, turned, table_here, slots_here, arrived, left
):
    rows, contracted = tau_ref.shape
    tiles = contracted // LANES
    table_copy = pltpu.make_async_copy(table_ref, table_here, arrived.at[2 * tiles])
    table_copy.start()
    incoming = []
    for tile in range(tiles):
        lanes = pl.ds(tile * LANES, LANES)
        for part, source in enumerate((tau_ref, lambda_ref)):
            incoming.append(
                pltpu.make_async_copy(
                    source.at[:, lanes],
                    both.at[tile, pl.ds(part * rows, rows)],
                    arrived.at[2 * tile + part],
                )
            )
    for copy in incoming:
        copy.start()
    table_copy.wait()
    slots_here[...] = partner_slots(table_here[...], slots_here.shape)
    slots_copy = pltpu.make_async_copy(slots_here, slots_ref, left.at[tiles])
    slots_copy.start()
    outgoing = [slots_copy]
    for tile in range(tiles):
        incoming[2 * tile].wait()
        incoming[2 * tile + 1].wait()
        turned[tile] = both[tile].T
        copy = pltpu.make_async_copy(
            turned.at[tile], packed_ref.at[pl.ds(tile * LANES, LANES)], left.at[tile]
        )
        copy.start()
        outgoing.append(copy)
    for copy in outgoing:
        copy.wait()


def pack(tau_rows, lambda_rows, table):
    rows, contracted = tau_rows.shape
    tiles = contracted // LANES
    return pl.pallas_call(
        pack_kernel,
        out_shape=(
            jax.ShapeDtypeStruct((contracted, 2 * rows), jnp.bfloat16),
            jax.ShapeDtypeStruct((table.shape[0], LANES), jnp.int32),
        ),
        in_specs=[pl.BlockSpec(memory_space=pltpu.HBM)] * 3,
        out_specs=(pl.BlockSpec(memory_space=pltpu.HBM),) * 2,
        scratch_shapes=[
            pltpu.VMEM((tiles, 2 * rows, LANES), jnp.bfloat16),
            pltpu.VMEM((tiles, LANES, 2 * rows), jnp.bfloat16),
            pltpu.VMEM(table.shape, jnp.int32),
            pltpu.VMEM((table.shape[0], LANES), jnp.int32),
            pltpu.SemaphoreType.DMA((2 * tiles + 1,)),
            pltpu.SemaphoreType.DMA((tiles + 1,)),
        ],
        compiler_params=pltpu.CompilerParams(vmem_limit_bytes=56 * 2**20),
        name="pack",
    )(tau_rows, lambda_rows, table)


def pair_kernel(
    virtuals, slots_ref, packed_ref, out_ref, tau_part, lambda_part, chosen, slots, arrived
):
    slots_copy = pltpu.make_async_copy(slots_ref, slots, arrived)
    slots_copy.start()
    groups, depth, width = packed_ref.shape
    triples = 2 * groups
    slot_rows = tau_part.shape[1]
    qcount = 2
    half = width // 2
    fill = jnp.zeros((slot_rows - depth, half), jnp.float32)
    lane_fill = jnp.zeros((slot_rows, LANES - virtuals), jnp.bfloat16)
    for group in range(groups):
        block = packed_ref[group].astype(jnp.float32)
        tau_block = jnp.concatenate([block[:, :half], fill], 0).astype(jnp.bfloat16)
        lambda_block = jnp.concatenate([block[:, half:], fill], 0).astype(jnp.bfloat16)
        for local_triple in range(2):
            start = local_triple * 2 * virtuals
            tau_part[2 * group + local_triple] = tau_block[:, start : start + 2 * virtuals]
            lambda_part[2 * group + local_triple] = jnp.concatenate(
                [
                    lambda_block[:, start : start + virtuals],
                    lane_fill,
                    lambda_block[:, start + virtuals : start + 2 * virtuals],
                    lane_fill,
                ],
                1,
            )

    slots_copy.wait()

    def choose(slot, triple):
        value = lambda_part[slots[triple, slot]]
        transfer = slots[triple, 2 + slot]
        for q in range(qcount):
            chosen[slot, triple, :, q * 2 * LANES : (q + 1) * 2 * LANES] = jnp.where(
                transfer == q, value, jnp.zeros_like(value)
            )

    for triple in range(triples):
        choose(0, triple)
        choose(1, triple)
    tau_all = tau_part[...].reshape(triples * slot_rows, 2 * virtuals)
    total = jnp.zeros((2 * virtuals, qcount * 2 * LANES), jnp.float32)
    for slot in range(2):
        total += lax.dot_general(
            tau_all,
            chosen[slot].reshape(triples * slot_rows, qcount * 2 * LANES),
            (((0,), (0,)), ((), ())),
            preferred_element_type=jnp.float32,
        )
    owned = virtuals // groups
    blank = jnp.zeros((SUBLANES - owned, LANES), jnp.float32)
    for q in range(qcount):
        lane = q * 2 * LANES
        real_lambda = total[:, lane : lane + LANES]
        imag_lambda = total[:, lane + LANES : lane + 2 * LANES]
        real_part = real_lambda[:virtuals] + imag_lambda[virtuals:]
        imag_part = real_lambda[virtuals:] - imag_lambda[:virtuals]
        for place, part in ((2 * q, real_part), (2 * q + 1, imag_part)):
            for group in range(groups):
                out_ref[group, place * SUBLANES : (place + 1) * SUBLANES] = jnp.concatenate(
                    [part[group * owned : (group + 1) * owned], blank], 0
                )


def pair_terms(slots, packed, virtuals):
    groups, depth, width = packed.shape
    slot_rows = -(-depth // 16) * 16
    triples = 2 * groups
    return pl.pallas_call(
        lambda *refs: pair_kernel(virtuals, *refs),
        out_shape=jax.ShapeDtypeStruct((groups, 4 * SUBLANES, LANES), jnp.float32),
        in_specs=[pl.BlockSpec(memory_space=pl.ANY), pl.BlockSpec(memory_space=pltpu.VMEM)],
        out_specs=pl.BlockSpec(memory_space=pltpu.VMEM),
        scratch_shapes=[
            pltpu.VMEM((triples, slot_rows, 2 * virtuals), jnp.bfloat16),
            pltpu.VMEM((triples, slot_rows, 2 * LANES), jnp.bfloat16),
            pltpu.VMEM((2, triples, slot_rows, 4 * LANES), jnp.bfloat16),
            pltpu.SMEM(slots.shape, jnp.int32),
            pltpu.SemaphoreType.DMA,
        ],
        compiler_params=pltpu.CompilerParams(vmem_limit_bytes=40 * 2**20),
        name="pairs",
    )(slots, packed)


def factor_kernel(far, parts_ref, factors_ref, out_ref):
    qcount, depth, _ = factors_ref.shape
    owned = out_ref.shape[1]
    virtuals = depth // 2
    for q in range(qcount):
        density = []
        for component in range(2):
            total = parts_ref[q * far * 2 + component]
            for step in range(1, far):
                total += parts_ref[(q * far + step) * 2 + component]
            density.append(total[:, :virtuals].astype(jnp.bfloat16).astype(jnp.float32))
        real, imag = density
        upper = jnp.concatenate([real, -imag], 1)
        lower = jnp.concatenate([imag, real], 1)
        rows = jnp.concatenate([upper, lower], 0).astype(jnp.bfloat16)
        gamma = jnp.dot(rows, factors_ref[q], preferred_element_type=jnp.float32)
        for row in range(owned):
            out_ref[q, row] = jnp.concatenate(
                [gamma[row : row + 1], gamma[SUBLANES + row : SUBLANES + row + 1]], 0
            )


def factor_product(parts, factors, owned, far):
    qcount, _, columns = factors.shape
    return pl.pallas_call(
        lambda *refs: factor_kernel(far, *refs),
        out_shape=jax.ShapeDtypeStruct((qcount, owned, 2, columns), jnp.float32),
        in_specs=[pl.BlockSpec(memory_space=pltpu.VMEM)] * 2,
        out_specs=pl.BlockSpec(memory_space=pltpu.VMEM),
        compiler_params=pltpu.CompilerParams(vmem_limit_bytes=24 * 2**20),
        name="factors",
    )(parts, factors)


def local(tau_slabs, lambda_slabs, aux_factor, transfer_table):
    groups = lax.axis_size("kring")
    virtuals = tau_slabs.shape[2]
    contracted = tau_slabs.shape[3]
    qcount = aux_factor.shape[0]
    rows = tau_slabs.shape[0] * 2 * virtuals
    owned = virtuals // groups
    packed, slots = pack(
        tau_slabs.reshape(rows, contracted), lambda_slabs.reshape(rows, contracted), transfer_table
    )
    packed = packed.reshape(groups, contracted // groups, 2 * rows)
    exchanged = lax.all_to_all(packed, "kring", 0, 0)
    partial = pair_terms(slots, exchanged, virtuals)
    near = ("kring", "y_lo", "z_lo")
    orb = ("y_lo", "z_hi", "z_lo")
    tiles = partial.reshape(lax.axis_size(near), SUBLANES, LANES)
    tile = lax.all_to_all(tiles, near, 0, 0).sum(0)
    copies = jnp.broadcast_to(tile[None], (lax.axis_size(orb),) + tile.shape)
    parts = lax.all_to_all(copies, orb, 0, 0)
    factors = aux_factor.reshape(qcount, 2 * virtuals, aux_factor.shape[3])
    gamma = factor_product(parts, factors, owned, lax.axis_size("z_hi"))
    return gamma.transpose(0, 2, 1, 3)


def solution(mesh):
    groups, spread = mesh.devices.shape
    parts = jax.sharding.Mesh(
        mesh.devices.reshape(groups, 2, spread // 4, 2), ("kring", "y_lo", "z_hi", "z_lo")
    )
    orb = ("y_lo", "z_hi", "z_lo")
    in_specs = (
        P("kring", None, None, orb),
        P("kring", None, None, orb),
        P(None, None, None, orb),
        P(),
    )
    out_specs = P(None, None, "kring", orb)
    return jax.shard_map(local, mesh=parts, in_specs=in_specs, out_specs=out_specs, check_vma=False)
```

```python
import jax
import jax.numpy as jnp
from jax import lax
from jax.experimental import pallas as pl
from jax.experimental.pallas import tpu as pltpu
from jax.sharding import PartitionSpec as P

LANES = 128
SUBLANES = 8


def partner_slots(table, shape):
    none = 2
    column = lax.broadcasted_iota(jnp.int32, table.shape, 1)
    used = table != none
    first = jnp.min(jnp.where(used, column, table.shape[1] - 1), 1, keepdims=True)
    last = jnp.max(jnp.where(used, column, 0), 1, keepdims=True)
    first_q = jnp.sum(jnp.where(column == first, table, 0), 1, keepdims=True)
    last_q = jnp.sum(jnp.where(column == last, table, 0), 1, keepdims=True)
    last_q = jnp.where(last == first, none, last_q)
    place = lax.broadcasted_iota(jnp.int32, shape, 1)
    return jnp.where(
        place == 0, first, jnp.where(place == 1, last, jnp.where(place == 2, first_q, last_q))
    )


def pack_kernel(
    tau_ref, lambda_ref, table_ref, packed_ref, slots_ref, both, turned, table_here, slots_here, arrived, left
):
    rows, contracted = tau_ref.shape
    tiles = contracted // LANES
    table_copy = pltpu.make_async_copy(table_ref, table_here, arrived.at[2 * tiles])
    table_copy.start()
    incoming = []
    for tile in range(tiles):
        lanes = pl.ds(tile * LANES, LANES)
        for part, source in enumerate((tau_ref, lambda_ref)):
            incoming.append(
                pltpu.make_async_copy(
                    source.at[:, lanes],
                    both.at[tile, pl.ds(part * rows, rows)],
                    arrived.at[2 * tile + part],
                )
            )
    for copy in incoming:
        copy.start()
    table_copy.wait()
    slots_here[...] = partner_slots(table_here[...], slots_here.shape)
    slots_copy = pltpu.make_async_copy(slots_here, slots_ref, left.at[tiles])
    slots_copy.start()
    outgoing = [slots_copy]
    for tile in range(tiles):
        incoming[2 * tile].wait()
        incoming[2 * tile + 1].wait()
        turned[tile] = both[tile].T
        copy = pltpu.make_async_copy(
            turned.at[tile], packed_ref.at[pl.ds(tile * LANES, LANES)], left.at[tile]
        )
        copy.start()
        outgoing.append(copy)
    for copy in outgoing:
        copy.wait()


def pack(tau_rows, lambda_rows, table):
    rows, contracted = tau_rows.shape
    tiles = contracted // LANES
    return pl.pallas_call(
        pack_kernel,
        out_shape=(
            jax.ShapeDtypeStruct((contracted, 2 * rows), jnp.bfloat16),
            jax.ShapeDtypeStruct((table.shape[0], LANES), jnp.int32),
        ),
        in_specs=[pl.BlockSpec(memory_space=pltpu.HBM)] * 3,
        out_specs=(pl.BlockSpec(memory_space=pltpu.HBM),) * 2,
        scratch_shapes=[
            pltpu.VMEM((tiles, 2 * rows, LANES), jnp.bfloat16),
            pltpu.VMEM((tiles, LANES, 2 * rows), jnp.bfloat16),
            pltpu.VMEM(table.shape, jnp.int32),
            pltpu.VMEM((table.shape[0], LANES), jnp.int32),
            pltpu.SemaphoreType.DMA((2 * tiles + 1,)),
            pltpu.SemaphoreType.DMA((tiles + 1,)),
        ],
        compiler_params=pltpu.CompilerParams(vmem_limit_bytes=56 * 2**20),
        name="pack",
    )(tau_rows, lambda_rows, table)


def pair_kernel(
    virtuals, slots_ref, packed_ref, out_ref, tau_part, lambda_part, chosen, slots, arrived
):
    slots_copy = pltpu.make_async_copy(slots_ref, slots, arrived)
    slots_copy.start()
    groups, depth, width = packed_ref.shape
    triples = 2 * groups
    slot_rows = tau_part.shape[1]
    qcount = 2
    half = width // 2
    fill = jnp.zeros((slot_rows - depth, half), jnp.float32)
    lane_fill = jnp.zeros((slot_rows, LANES - virtuals), jnp.bfloat16)
    for group in range(groups):
        block = packed_ref[group].astype(jnp.float32)
        tau_block = jnp.concatenate([block[:, :half], fill], 0).astype(jnp.bfloat16)
        lambda_block = jnp.concatenate([block[:, half:], fill], 0).astype(jnp.bfloat16)
        for local_triple in range(2):
            start = local_triple * 2 * virtuals
            tau_part[2 * group + local_triple] = tau_block[:, start : start + 2 * virtuals]
            lambda_part[2 * group + local_triple] = jnp.concatenate(
                [
                    lambda_block[:, start : start + virtuals],
                    lane_fill,
                    lambda_block[:, start + virtuals : start + 2 * virtuals],
                    lane_fill,
                ],
                1,
            )

    slots_copy.wait()

    def choose(slot, triple):
        value = lambda_part[slots[triple, slot]]
        transfer = slots[triple, 2 + slot]
        for q in range(qcount):
            chosen[slot, triple, :, q * 2 * LANES : (q + 1) * 2 * LANES] = jnp.where(
                transfer == q, value, jnp.zeros_like(value)
            )

    for triple in range(triples):
        choose(0, triple)
        choose(1, triple)
    tau_all = tau_part[...].reshape(triples * slot_rows, 2 * virtuals)
    total = jnp.zeros((2 * virtuals, qcount * 2 * LANES), jnp.float32)
    for slot in range(2):
        total += lax.dot_general(
            tau_all,
            chosen[slot].reshape(triples * slot_rows, qcount * 2 * LANES),
            (((0,), (0,)), ((), ())),
            preferred_element_type=jnp.float32,
        )
    owned = virtuals // groups
    blank = jnp.zeros((SUBLANES - owned, LANES), jnp.float32)
    for q in range(qcount):
        lane = q * 2 * LANES
        real_lambda = total[:, lane : lane + LANES]
        imag_lambda = total[:, lane + LANES : lane + 2 * LANES]
        real_part = real_lambda[:virtuals] + imag_lambda[virtuals:]
        imag_part = real_lambda[virtuals:] - imag_lambda[:virtuals]
        for place, part in ((2 * q, real_part), (2 * q + 1, imag_part)):
            for group in range(groups):
                out_ref[group, place * SUBLANES : (place + 1) * SUBLANES] = jnp.concatenate(
                    [part[group * owned : (group + 1) * owned], blank], 0
                )


def pair_terms(slots, packed, virtuals):
    groups, depth, width = packed.shape
    slot_rows = -(-depth // 16) * 16
    triples = 2 * groups
    return pl.pallas_call(
        lambda *refs: pair_kernel(virtuals, *refs),
        out_shape=jax.ShapeDtypeStruct((groups, 4 * SUBLANES, LANES), jnp.float32),
        in_specs=[pl.BlockSpec(memory_space=pl.ANY), pl.BlockSpec(memory_space=pltpu.VMEM)],
        out_specs=pl.BlockSpec(memory_space=pltpu.VMEM),
        scratch_shapes=[
            pltpu.VMEM((triples, slot_rows, 2 * virtuals), jnp.bfloat16),
            pltpu.VMEM((triples, slot_rows, 2 * LANES), jnp.bfloat16),
            pltpu.VMEM((2, triples, slot_rows, 4 * LANES), jnp.bfloat16),
            pltpu.SMEM(slots.shape, jnp.int32),
            pltpu.SemaphoreType.DMA,
        ],
        compiler_params=pltpu.CompilerParams(vmem_limit_bytes=40 * 2**20),
        name="pairs",
    )(slots, packed)


def factor_kernel(far, parts_ref, factors_ref, out_ref):
    qcount, depth, _ = factors_ref.shape
    owned = out_ref.shape[1]
    virtuals = depth // 2
    for q in range(qcount):
        density = []
        for component in range(2):
            total = parts_ref[q * far * 2 + component].astype(jnp.float32)
            for step in range(1, far):
                total += parts_ref[(q * far + step) * 2 + component].astype(jnp.float32)
            density.append(total[:, :virtuals])
        real, imag = density
        upper = jnp.concatenate([real, -imag], 1)
        lower = jnp.concatenate([imag, real], 1)
        rows = jnp.concatenate([upper, lower], 0)
        high = rows.astype(jnp.bfloat16)
        low = (rows - high.astype(jnp.float32)).astype(jnp.bfloat16)
        both = jnp.concatenate([high, low], 0)
        gamma = jnp.dot(both, factors_ref[q], preferred_element_type=jnp.float32)
        gamma = gamma[: 2 * SUBLANES] + gamma[2 * SUBLANES :]
        for row in range(owned):
            out_ref[q, row] = jnp.concatenate(
                [gamma[row : row + 1], gamma[SUBLANES + row : SUBLANES + row + 1]], 0
            )


def factor_product(parts, factors, owned, far):
    qcount, _, columns = factors.shape
    return pl.pallas_call(
        lambda *refs: factor_kernel(far, *refs),
        out_shape=jax.ShapeDtypeStruct((qcount, owned, 2, columns), jnp.float32),
        in_specs=[pl.BlockSpec(memory_space=pltpu.VMEM)] * 2,
        out_specs=pl.BlockSpec(memory_space=pltpu.VMEM),
        compiler_params=pltpu.CompilerParams(vmem_limit_bytes=24 * 2**20),
        name="factors",
    )(parts, factors)


def local(tau_slabs, lambda_slabs, aux_factor, transfer_table):
    groups = lax.axis_size("kring")
    virtuals = tau_slabs.shape[2]
    contracted = tau_slabs.shape[3]
    qcount = aux_factor.shape[0]
    rows = tau_slabs.shape[0] * 2 * virtuals
    owned = virtuals // groups
    packed, slots = pack(
        tau_slabs.reshape(rows, contracted), lambda_slabs.reshape(rows, contracted), transfer_table
    )
    packed = packed.reshape(groups, contracted // groups, 2 * rows)
    exchanged = lax.all_to_all(packed, "kring", 0, 0)
    partial = pair_terms(slots, exchanged, virtuals)
    near = ("kring", "y_lo", "z_lo")
    orb = ("y_lo", "z_hi", "z_lo")
    tiles = partial.reshape(lax.axis_size(near), SUBLANES, LANES)
    tile = lax.all_to_all(tiles, near, 0, 0).sum(0)
    tile = tile.astype(jnp.bfloat16)
    copies = jnp.broadcast_to(tile[None], (lax.axis_size(orb),) + tile.shape)
    half = lax.axis_size(orb) // 4
    order = [[*range(half, 2 * half), *range(half), *range(2 * half, 4 * half)]]
    parts = lax.all_to_all(copies, orb, 0, 0, axis_index_groups=order)
    factors = aux_factor.reshape(qcount, 2 * virtuals, aux_factor.shape[3])
    gamma = factor_product(parts, factors, owned, lax.axis_size("z_hi"))
    return gamma.transpose(0, 2, 1, 3)


def solution(mesh):
    groups, spread = mesh.devices.shape
    parts = jax.sharding.Mesh(
        mesh.devices.reshape(groups, 2, spread // 4, 2), ("kring", "y_lo", "z_hi", "z_lo")
    )
    orb = ("y_lo", "z_hi", "z_lo")
    in_specs = (
        P("kring", None, None, orb),
        P("kring", None, None, orb),
        P(None, None, None, orb),
        P(),
    )
    out_specs = P(None, None, "kring", orb)
    return jax.shard_map(local, mesh=parts, in_specs=in_specs, out_specs=out_specs, check_vma=False)
```

```python
import jax
import jax.numpy as jnp
from jax import lax
from jax.experimental import pallas as pl
from jax.experimental.pallas import tpu as pltpu
from jax.sharding import PartitionSpec as P

LANES = 128
SUBLANES = 8


def partner_slots(table, shape):
    none = 2
    column = lax.broadcasted_iota(jnp.int32, table.shape, 1)
    used = table != none
    first = jnp.min(jnp.where(used, column, table.shape[1] - 1), 1, keepdims=True)
    last = jnp.max(jnp.where(used, column, 0), 1, keepdims=True)
    first_q = jnp.sum(jnp.where(column == first, table, 0), 1, keepdims=True)
    last_q = jnp.sum(jnp.where(column == last, table, 0), 1, keepdims=True)
    last_q = jnp.where(last == first, none, last_q)
    place = lax.broadcasted_iota(jnp.int32, shape, 1)
    return jnp.where(
        place == 0, first, jnp.where(place == 1, last, jnp.where(place == 2, first_q, last_q))
    )


def pack_kernel(
    tau_ref, lambda_ref, table_ref, packed_ref, slots_ref, both, turned, table_here, slots_here, arrived, left
):
    rows, contracted = tau_ref.shape
    tiles = contracted // LANES
    table_copy = pltpu.make_async_copy(table_ref, table_here, arrived.at[2 * tiles])
    table_copy.start()
    incoming = []
    for tile in range(tiles):
        lanes = pl.ds(tile * LANES, LANES)
        for part, source in enumerate((tau_ref, lambda_ref)):
            incoming.append(
                pltpu.make_async_copy(
                    source.at[:, lanes],
                    both.at[tile, pl.ds(part * rows, rows)],
                    arrived.at[2 * tile + part],
                )
            )
    for copy in incoming:
        copy.start()
    table_copy.wait()
    slots_here[...] = partner_slots(table_here[...], slots_here.shape)
    slots_copy = pltpu.make_async_copy(slots_here, slots_ref, left.at[tiles])
    slots_copy.start()
    outgoing = [slots_copy]
    for tile in range(tiles):
        incoming[2 * tile].wait()
        incoming[2 * tile + 1].wait()
        turned[tile] = both[tile].T
        copy = pltpu.make_async_copy(
            turned.at[tile], packed_ref.at[pl.ds(tile * LANES, LANES)], left.at[tile]
        )
        copy.start()
        outgoing.append(copy)
    for copy in outgoing:
        copy.wait()


def pack(tau_rows, lambda_rows, table):
    rows, contracted = tau_rows.shape
    tiles = contracted // LANES
    return pl.pallas_call(
        pack_kernel,
        out_shape=(
            jax.ShapeDtypeStruct((contracted, 2 * rows), jnp.bfloat16),
            jax.ShapeDtypeStruct((table.shape[0], LANES), jnp.int32),
        ),
        in_specs=[pl.BlockSpec(memory_space=pltpu.HBM)] * 3,
        out_specs=(pl.BlockSpec(memory_space=pltpu.HBM),) * 2,
        scratch_shapes=[
            pltpu.VMEM((tiles, 2 * rows, LANES), jnp.bfloat16),
            pltpu.VMEM((tiles, LANES, 2 * rows), jnp.bfloat16),
            pltpu.VMEM(table.shape, jnp.int32),
            pltpu.VMEM((table.shape[0], LANES), jnp.int32),
            pltpu.SemaphoreType.DMA((2 * tiles + 1,)),
            pltpu.SemaphoreType.DMA((tiles + 1,)),
        ],
        compiler_params=pltpu.CompilerParams(vmem_limit_bytes=56 * 2**20),
        name="pack",
    )(tau_rows, lambda_rows, table)


def pair_kernel(
    virtuals, ring, slots_ref, packed_ref, out_ref, tau_part, lambda_part, chosen, slots, arrived
):
    slots_copy = pltpu.make_async_copy(slots_ref, slots, arrived)
    slots_copy.start()
    groups, depth, width = packed_ref.shape
    triples = 2 * groups
    slot_rows = tau_part.shape[1]
    qcount = 2
    half = width // 2
    fill = jnp.zeros((slot_rows - depth, half), jnp.float32)
    lane_fill = jnp.zeros((slot_rows, LANES - virtuals), jnp.bfloat16)
    for place, group in enumerate(ring):
        block = packed_ref[place].astype(jnp.float32)
        tau_block = jnp.concatenate([block[:, :half], fill], 0).astype(jnp.bfloat16)
        lambda_block = jnp.concatenate([block[:, half:], fill], 0).astype(jnp.bfloat16)
        for local_triple in range(2):
            start = local_triple * 2 * virtuals
            tau_part[2 * group + local_triple] = tau_block[:, start : start + 2 * virtuals]
            lambda_part[2 * group + local_triple] = jnp.concatenate(
                [
                    lambda_block[:, start : start + virtuals],
                    lane_fill,
                    lambda_block[:, start + virtuals : start + 2 * virtuals],
                    lane_fill,
                ],
                1,
            )

    slots_copy.wait()

    def choose(slot, triple):
        value = lambda_part[slots[triple, slot]]
        transfer = slots[triple, 2 + slot]
        for q in range(qcount):
            chosen[slot, triple, :, q * 2 * LANES : (q + 1) * 2 * LANES] = jnp.where(
                transfer == q, value, jnp.zeros_like(value)
            )

    for triple in range(triples):
        choose(0, triple)
        choose(1, triple)
    tau_all = tau_part[...].reshape(triples * slot_rows, 2 * virtuals)
    total = jnp.zeros((2 * virtuals, qcount * 2 * LANES), jnp.float32)
    for slot in range(2):
        total += lax.dot_general(
            tau_all,
            chosen[slot].reshape(triples * slot_rows, qcount * 2 * LANES),
            (((0,), (0,)), ((), ())),
            preferred_element_type=jnp.float32,
        )
    owned = virtuals // groups
    blank = jnp.zeros((SUBLANES - owned, LANES), jnp.float32)
    for q in range(qcount):
        lane = q * 2 * LANES
        real_lambda = total[:, lane : lane + LANES]
        imag_lambda = total[:, lane + LANES : lane + 2 * LANES]
        real_part = real_lambda[:virtuals] + imag_lambda[virtuals:]
        imag_part = real_lambda[virtuals:] - imag_lambda[:virtuals]
        for component, part in enumerate((real_part, imag_part)):
            row = (2 * q + component) * SUBLANES
            for place, group in enumerate(ring):
                out_ref[place, row : row + SUBLANES] = jnp.concatenate(
                    [part[group * owned : (group + 1) * owned], blank], 0
                )


def pair_terms(slots, packed, virtuals, ring):
    groups, depth, width = packed.shape
    slot_rows = -(-depth // 16) * 16
    triples = 2 * groups
    return pl.pallas_call(
        lambda *refs: pair_kernel(virtuals, ring, *refs),
        out_shape=jax.ShapeDtypeStruct((groups, 4 * SUBLANES, LANES), jnp.float32),
        in_specs=[pl.BlockSpec(memory_space=pl.ANY), pl.BlockSpec(memory_space=pltpu.VMEM)],
        out_specs=pl.BlockSpec(memory_space=pltpu.VMEM),
        scratch_shapes=[
            pltpu.VMEM((triples, slot_rows, 2 * virtuals), jnp.bfloat16),
            pltpu.VMEM((triples, slot_rows, 2 * LANES), jnp.bfloat16),
            pltpu.VMEM((2, triples, slot_rows, 4 * LANES), jnp.bfloat16),
            pltpu.SMEM(slots.shape, jnp.int32),
            pltpu.SemaphoreType.DMA,
        ],
        compiler_params=pltpu.CompilerParams(vmem_limit_bytes=40 * 2**20),
        name="pairs",
    )(slots, packed)


def factor_kernel(far, parts_ref, factors_ref, out_ref):
    qcount, depth, _ = factors_ref.shape
    owned = out_ref.shape[1]
    virtuals = depth // 2
    for q in range(qcount):
        density = []
        for component in range(2):
            total = parts_ref[q * far * 2 + component].astype(jnp.float32)
            for step in range(1, far):
                total += parts_ref[(q * far + step) * 2 + component].astype(jnp.float32)
            density.append(total[:, :virtuals])
        real, imag = density
        upper = jnp.concatenate([real, -imag], 1)
        lower = jnp.concatenate([imag, real], 1)
        rows = jnp.concatenate([upper, lower], 0)
        high = rows.astype(jnp.bfloat16)
        low = (rows - high.astype(jnp.float32)).astype(jnp.bfloat16)
        both = jnp.concatenate([high, low], 0)
        gamma = jnp.dot(both, factors_ref[q], preferred_element_type=jnp.float32)
        gamma = gamma[: 2 * SUBLANES] + gamma[2 * SUBLANES :]
        for row in range(owned):
            out_ref[q, row] = jnp.concatenate(
                [gamma[row : row + 1], gamma[SUBLANES + row : SUBLANES + row + 1]], 0
            )


def factor_product(parts, factors, owned, far):
    qcount, _, columns = factors.shape
    return pl.pallas_call(
        lambda *refs: factor_kernel(far, *refs),
        out_shape=jax.ShapeDtypeStruct((qcount, owned, 2, columns), jnp.float32),
        in_specs=[pl.BlockSpec(memory_space=pltpu.VMEM)] * 2,
        out_specs=pl.BlockSpec(memory_space=pltpu.VMEM),
        compiler_params=pltpu.CompilerParams(vmem_limit_bytes=24 * 2**20),
        name="factors",
    )(parts, factors)


def local(tau_slabs, lambda_slabs, aux_factor, transfer_table):
    groups = lax.axis_size("kring")
    virtuals = tau_slabs.shape[2]
    contracted = tau_slabs.shape[3]
    qcount = aux_factor.shape[0]
    rows = tau_slabs.shape[0] * 2 * virtuals
    owned = virtuals // groups
    packed, slots = pack(
        tau_slabs.reshape(rows, contracted), lambda_slabs.reshape(rows, contracted), transfer_table
    )
    packed = packed.reshape(groups, contracted // groups, 2 * rows)
    start = groups - groups // 4
    ring = [*range(start, groups), *range(start)]
    exchanged = lax.all_to_all(packed, "kring", 0, 0, axis_index_groups=[ring])
    partial = pair_terms(slots, exchanged, virtuals, ring)
    near = ("kring", "y_lo", "z_lo")
    orb = ("y_lo", "z_hi", "z_lo")
    pieces = lax.axis_size(near) // groups
    members = [[group * pieces + piece for group in ring for piece in range(pieces)]]
    tiles = partial.reshape(lax.axis_size(near), SUBLANES, LANES)
    tile = lax.all_to_all(tiles, near, 0, 0, axis_index_groups=members).sum(0)
    tile = tile.astype(jnp.bfloat16)
    copies = jnp.broadcast_to(tile[None], (lax.axis_size(orb),) + tile.shape)
    half = lax.axis_size(orb) // 4
    order = [[*range(half, 2 * half), *range(half), *range(2 * half, 4 * half)]]
    parts = lax.all_to_all(copies, orb, 0, 0, axis_index_groups=order)
    factors = aux_factor.reshape(qcount, 2 * virtuals, aux_factor.shape[3])
    gamma = factor_product(parts, factors, owned, lax.axis_size("z_hi"))
    return gamma.transpose(0, 2, 1, 3)


def solution(mesh):
    groups, spread = mesh.devices.shape
    parts = jax.sharding.Mesh(
        mesh.devices.reshape(groups, 2, spread // 4, 2), ("kring", "y_lo", "z_hi", "z_lo")
    )
    orb = ("y_lo", "z_hi", "z_lo")
    in_specs = (
        P("kring", None, None, orb),
        P("kring", None, None, orb),
        P(None, None, None, orb),
        P(),
    )
    out_specs = P(None, None, "kring", orb)
    return jax.shard_map(local, mesh=parts, in_specs=in_specs, out_specs=out_specs, check_vma=False)
```

```python
import jax
import jax.numpy as jnp
from jax import lax
from jax.experimental import pallas as pl
from jax.experimental.pallas import tpu as pltpu
from jax.sharding import PartitionSpec as P

LANES = 128
SUBLANES = 8


def partner_slots(table, shape):
    none = 2
    column = lax.broadcasted_iota(jnp.int32, table.shape, 1)
    used = table != none
    first = jnp.min(jnp.where(used, column, table.shape[1] - 1), 1, keepdims=True)
    last = jnp.max(jnp.where(used, column, 0), 1, keepdims=True)
    first_q = jnp.sum(jnp.where(column == first, table, 0), 1, keepdims=True)
    last_q = jnp.sum(jnp.where(column == last, table, 0), 1, keepdims=True)
    last_q = jnp.where(last == first, none, last_q)
    place = lax.broadcasted_iota(jnp.int32, shape, 1)
    return jnp.where(
        place == 0, first, jnp.where(place == 1, last, jnp.where(place == 2, first_q, last_q))
    )


def pack_kernel(
    virtuals, tau_ref, lambda_ref, table_ref, packed_ref, slots_ref, both, turned, table_here,
    slots_here, arrived, left
):
    contracted = both.shape[1]
    tiles = both.shape[0] // LANES
    spare = LANES - virtuals
    whole = [(lambda_ref, at) for at in range(4)] + [(tau_ref, at) for at in range(3)]
    moves = [(source, at * virtuals, tile * LANES, virtuals) for tile, (source, at) in enumerate(whole)]
    for tile in range(tiles):
        moves.append((tau_ref, 3 * virtuals + tile * spare, tile * LANES + virtuals, spare))
    incoming = []
    for number, (source, start, place, size) in enumerate(moves):
        incoming.append(
            pltpu.make_async_copy(
                source.at[pl.ds(start, size)], both.at[pl.ds(place, size)], arrived.at[number]
            )
        )
    table_copy = pltpu.make_async_copy(table_ref, table_here, arrived.at[len(moves)])
    table_copy.start()
    for copy in incoming:
        copy.start()
    table_copy.wait()
    slots_here[...] = partner_slots(table_here[...], slots_here.shape)
    slots_copy = pltpu.make_async_copy(slots_here, slots_ref, left.at[tiles])
    slots_copy.start()
    outgoing = [slots_copy]
    for copy in incoming:
        copy.wait()
    for tile in range(contracted // LANES):
        start = tile * LANES
        turned[start : start + LANES] = both[:, start : start + LANES].T
        copy = pltpu.make_async_copy(
            turned.at[pl.ds(start, LANES)], packed_ref.at[pl.ds(start, LANES)], left.at[tile]
        )
        copy.start()
        outgoing.append(copy)
    for copy in outgoing:
        copy.wait()


def pack(tau_rows, lambda_rows, table, virtuals):
    rows, contracted = tau_rows.shape
    tiles = 2 * rows // LANES
    return pl.pallas_call(
        lambda *refs: pack_kernel(virtuals, *refs),
        out_shape=(
            jax.ShapeDtypeStruct((contracted, 2 * rows), jnp.bfloat16),
            jax.ShapeDtypeStruct((table.shape[0], LANES), jnp.int32),
        ),
        in_specs=[pl.BlockSpec(memory_space=pltpu.HBM)] * 3,
        out_specs=(pl.BlockSpec(memory_space=pltpu.HBM),) * 2,
        scratch_shapes=[
            pltpu.VMEM((2 * rows, contracted), jnp.bfloat16),
            pltpu.VMEM((contracted, 2 * rows), jnp.bfloat16),
            pltpu.VMEM(table.shape, jnp.int32),
            pltpu.VMEM((table.shape[0], LANES), jnp.int32),
            pltpu.SemaphoreType.DMA((2 * tiles + 1,)),
            pltpu.SemaphoreType.DMA((tiles + 1,)),
        ],
        compiler_params=pltpu.CompilerParams(vmem_limit_bytes=56 * 2**20),
        name="pack",
    )(tau_rows, lambda_rows, table)


def pair_kernel(
    virtuals, ring, slots_ref, packed_ref, out_ref, tau_part, chosen, slots, arrived
):
    slots_copy = pltpu.make_async_copy(slots_ref, slots, arrived)
    slots_copy.start()
    groups, depth, width = packed_ref.shape
    triples = 2 * groups
    slot_rows = tau_part.shape[1]
    qcount = 2
    pair = 2 * LANES
    spare = LANES - virtuals
    fill = jnp.zeros((slot_rows - depth, pair), jnp.bfloat16)

    def deep(value):
        return jnp.concatenate([value, fill], 0)

    for place, group in enumerate(ring):
        tau_part[2 * group] = deep(packed_ref[place, :, 2 * pair : 3 * pair])
        scattered = [
            packed_ref[place, :, tile * LANES + virtuals : (tile + 1) * LANES]
            for tile in range(width // LANES)
        ]
        last = packed_ref[place, :, 3 * pair : 3 * pair + LANES]
        unused = jnp.zeros((depth, spare), jnp.bfloat16)
        tau_part[2 * group + 1] = deep(jnp.concatenate([last] + scattered + [unused], 1))
    slots_copy.wait()
    for triple in range(triples):
        for slot in range(2):
            partner = slots[triple, slot]
            transfer = slots[triple, 2 + slot]
            place = lax.rem(partner // 2 + groups - ring[0], groups)
            value = jnp.where(
                partner % 2 == 0, packed_ref[place, :, :pair], packed_ref[place, :, pair : 2 * pair]
            )
            value = deep(value)
            for q in range(qcount):
                lane = (slot * qcount + q) * pair
                chosen[triple, :, lane : lane + pair] = jnp.where(
                    transfer == q, value, jnp.zeros_like(value)
                )
    wide = qcount * pair
    products = lax.dot_general(
        tau_part[...].reshape(triples * slot_rows, pair),
        chosen[...].reshape(triples * slot_rows, 2 * wide),
        (((0,), (0,)), ((), ())),
        preferred_element_type=jnp.float32,
    )
    total = products[:, :wide] + products[:, wide:]
    owned = virtuals // groups
    blank = jnp.zeros((SUBLANES - owned, LANES), jnp.float32)
    for q in range(qcount):
        lane = q * 2 * LANES
        real_lambda = total[:, lane : lane + LANES]
        imag_lambda = total[:, lane + LANES : lane + 2 * LANES]
        real_part = real_lambda[:LANES] + imag_lambda[LANES:]
        imag_part = real_lambda[LANES:] - imag_lambda[:LANES]
        for component, part in enumerate((real_part, imag_part)):
            row = (2 * q + component) * SUBLANES
            for place, group in enumerate(ring):
                out_ref[place, row : row + SUBLANES] = jnp.concatenate(
                    [part[group * owned : (group + 1) * owned], blank], 0
                )


def pair_terms(slots, packed, virtuals, ring):
    groups, depth, width = packed.shape
    slot_rows = -(-depth // 16) * 16
    triples = 2 * groups
    return pl.pallas_call(
        lambda *refs: pair_kernel(virtuals, ring, *refs),
        out_shape=jax.ShapeDtypeStruct((groups, 4 * SUBLANES, LANES), jnp.float32),
        in_specs=[pl.BlockSpec(memory_space=pl.ANY), pl.BlockSpec(memory_space=pltpu.VMEM)],
        out_specs=pl.BlockSpec(memory_space=pltpu.VMEM),
        scratch_shapes=[
            pltpu.VMEM((triples, slot_rows, 2 * LANES), jnp.bfloat16),
            pltpu.VMEM((triples, slot_rows, 8 * LANES), jnp.bfloat16),
            pltpu.SMEM(slots.shape, jnp.int32),
            pltpu.SemaphoreType.DMA,
        ],
        compiler_params=pltpu.CompilerParams(vmem_limit_bytes=40 * 2**20),
        name="pairs",
    )(slots, packed)


def factor_kernel(far, parts_ref, factors_ref, out_ref):
    qcount, depth, _ = factors_ref.shape
    owned = out_ref.shape[1]
    virtuals = depth // 2
    for q in range(qcount):
        density = []
        for component in range(2):
            total = parts_ref[q * far * 2 + component].astype(jnp.float32)
            for step in range(1, far):
                total += parts_ref[(q * far + step) * 2 + component].astype(jnp.float32)
            density.append(total[:, :virtuals])
        real, imag = density
        upper = jnp.concatenate([real, -imag], 1)
        lower = jnp.concatenate([imag, real], 1)
        rows = jnp.concatenate([upper, lower], 0)
        high = rows.astype(jnp.bfloat16)
        low = (rows - high.astype(jnp.float32)).astype(jnp.bfloat16)
        both = jnp.concatenate([high, low], 0)
        gamma = jnp.dot(both, factors_ref[q], preferred_element_type=jnp.float32)
        gamma = gamma[: 2 * SUBLANES] + gamma[2 * SUBLANES :]
        for row in range(owned):
            out_ref[q, row] = jnp.concatenate(
                [gamma[row : row + 1], gamma[SUBLANES + row : SUBLANES + row + 1]], 0
            )


def factor_product(parts, factors, owned, far):
    qcount, _, columns = factors.shape
    return pl.pallas_call(
        lambda *refs: factor_kernel(far, *refs),
        out_shape=jax.ShapeDtypeStruct((qcount, owned, 2, columns), jnp.float32),
        in_specs=[pl.BlockSpec(memory_space=pltpu.VMEM)] * 2,
        out_specs=pl.BlockSpec(memory_space=pltpu.VMEM),
        compiler_params=pltpu.CompilerParams(vmem_limit_bytes=24 * 2**20),
        name="factors",
    )(parts, factors)


def local(tau_slabs, lambda_slabs, aux_factor, transfer_table):
    groups = lax.axis_size("kring")
    virtuals = tau_slabs.shape[2]
    contracted = tau_slabs.shape[3]
    qcount = aux_factor.shape[0]
    rows = tau_slabs.shape[0] * 2 * virtuals
    owned = virtuals // groups
    packed, slots = pack(
        tau_slabs.reshape(rows, contracted), lambda_slabs.reshape(rows, contracted), transfer_table, virtuals
    )
    packed = packed.reshape(groups, contracted // groups, 2 * rows)
    start = groups - groups // 4
    ring = [*range(start, groups), *range(start)]
    exchanged = lax.all_to_all(packed, "kring", 0, 0, axis_index_groups=[ring])
    partial = pair_terms(slots, exchanged, virtuals, ring)
    near = ("kring", "y_lo", "z_lo")
    orb = ("y_lo", "z_hi", "z_lo")
    pieces = lax.axis_size(near) // groups
    members = [[group * pieces + piece for group in ring for piece in range(pieces)]]
    tiles = partial.reshape(lax.axis_size(near), SUBLANES, LANES)
    tile = lax.all_to_all(tiles, near, 0, 0, axis_index_groups=members).sum(0)
    tile = tile.astype(jnp.bfloat16)
    copies = jnp.broadcast_to(tile[None], (lax.axis_size(orb),) + tile.shape)
    half = lax.axis_size(orb) // 4
    order = [[*range(half, 2 * half), *range(half), *range(2 * half, 4 * half)]]
    parts = lax.all_to_all(copies, orb, 0, 0, axis_index_groups=order)
    factors = aux_factor.reshape(qcount, 2 * virtuals, aux_factor.shape[3])
    gamma = factor_product(parts, factors, owned, lax.axis_size("z_hi"))
    return gamma.transpose(0, 2, 1, 3)


def solution(mesh):
    groups, spread = mesh.devices.shape
    parts = jax.sharding.Mesh(
        mesh.devices.reshape(groups, 2, spread // 4, 2), ("kring", "y_lo", "z_hi", "z_lo")
    )
    orb = ("y_lo", "z_hi", "z_lo")
    in_specs = (
        P("kring", None, None, orb),
        P("kring", None, None, orb),
        P(None, None, None, orb),
        P(),
    )
    out_specs = P(None, None, "kring", orb)
    return jax.shard_map(local, mesh=parts, in_specs=in_specs, out_specs=out_specs, check_vma=False)
```

```python
import jax
import jax.numpy as jnp
from jax import lax
from jax.experimental import pallas as pl
from jax.experimental.pallas import tpu as pltpu
from jax.sharding import PartitionSpec as P

LANES = 128
SUBLANES = 8
SMALLEST = 2.0**-100
HEADROOM = 13.0


def partner_slots(table, shape):
    none = 2
    column = lax.broadcasted_iota(jnp.int32, table.shape, 1)
    used = table != none
    first = jnp.min(jnp.where(used, column, table.shape[1] - 1), 1, keepdims=True)
    last = jnp.max(jnp.where(used, column, 0), 1, keepdims=True)
    first_q = jnp.sum(jnp.where(column == first, table, 0), 1, keepdims=True)
    last_q = jnp.sum(jnp.where(column == last, table, 0), 1, keepdims=True)
    last_q = jnp.where(last == first, none, last_q)
    place = lax.broadcasted_iota(jnp.int32, shape, 1)
    return jnp.where(
        place == 0, first, jnp.where(place == 1, last, jnp.where(place == 2, first_q, last_q))
    )


def pack_kernel(
    tau_ref, lambda_ref, table_ref, packed_ref, slots_ref, both, turned, table_here, slots_here, arrived, left
):
    rows, contracted = tau_ref.shape
    tiles = contracted // LANES
    table_copy = pltpu.make_async_copy(table_ref, table_here, arrived.at[2 * tiles])
    table_copy.start()
    incoming = []
    for tile in range(tiles):
        lanes = pl.ds(tile * LANES, LANES)
        for part, source in enumerate((tau_ref, lambda_ref)):
            incoming.append(
                pltpu.make_async_copy(
                    source.at[:, lanes],
                    both.at[tile, pl.ds(part * rows, rows)],
                    arrived.at[2 * tile + part],
                )
            )
    for copy in incoming:
        copy.start()
    table_copy.wait()
    slots_here[...] = partner_slots(table_here[...], slots_here.shape)
    slots_copy = pltpu.make_async_copy(slots_here, slots_ref, left.at[tiles])
    slots_copy.start()
    outgoing = [slots_copy]
    for tile in range(tiles):
        incoming[2 * tile].wait()
        incoming[2 * tile + 1].wait()
        turned[tile] = both[tile].T
        copy = pltpu.make_async_copy(
            turned.at[tile], packed_ref.at[pl.ds(tile * LANES, LANES)], left.at[tile]
        )
        copy.start()
        outgoing.append(copy)
    for copy in outgoing:
        copy.wait()


def pack(tau_rows, lambda_rows, table):
    rows, contracted = tau_rows.shape
    tiles = contracted // LANES
    return pl.pallas_call(
        pack_kernel,
        out_shape=(
            jax.ShapeDtypeStruct((contracted, 2 * rows), jnp.bfloat16),
            jax.ShapeDtypeStruct((table.shape[0], LANES), jnp.int32),
        ),
        in_specs=[pl.BlockSpec(memory_space=pltpu.HBM)] * 3,
        out_specs=(pl.BlockSpec(memory_space=pltpu.HBM),) * 2,
        scratch_shapes=[
            pltpu.VMEM((tiles, 2 * rows, LANES), jnp.bfloat16),
            pltpu.VMEM((tiles, LANES, 2 * rows), jnp.bfloat16),
            pltpu.VMEM(table.shape, jnp.int32),
            pltpu.VMEM((table.shape[0], LANES), jnp.int32),
            pltpu.SemaphoreType.DMA((2 * tiles + 1,)),
            pltpu.SemaphoreType.DMA((tiles + 1,)),
        ],
        compiler_params=pltpu.CompilerParams(vmem_limit_bytes=56 * 2**20),
        name="pack",
    )(tau_rows, lambda_rows, table)


def pair_kernel(
    virtuals, ring, slots_ref, packed_ref, out_ref, tau_part, lambda_part, chosen, slots, arrived
):
    slots_copy = pltpu.make_async_copy(slots_ref, slots, arrived)
    slots_copy.start()
    groups, depth, width = packed_ref.shape
    triples = 2 * groups
    slot_rows = tau_part.shape[1]
    qcount = 2
    half = width // 2
    fill = jnp.zeros((slot_rows - depth, half), jnp.float32)
    lane_fill = jnp.zeros((slot_rows, LANES - virtuals), jnp.bfloat16)
    for place, group in enumerate(ring):
        block = packed_ref[place].astype(jnp.float32)
        tau_block = jnp.concatenate([block[:, :half], fill], 0).astype(jnp.bfloat16)
        lambda_block = jnp.concatenate([block[:, half:], fill], 0).astype(jnp.bfloat16)
        for local_triple in range(2):
            start = local_triple * 2 * virtuals
            tau_part[2 * group + local_triple] = tau_block[:, start : start + 2 * virtuals]
            lambda_part[2 * group + local_triple] = jnp.concatenate(
                [
                    lambda_block[:, start : start + virtuals],
                    lane_fill,
                    lambda_block[:, start + virtuals : start + 2 * virtuals],
                    lane_fill,
                ],
                1,
            )

    slots_copy.wait()

    def choose(slot, triple):
        value = lambda_part[slots[triple, slot]]
        transfer = slots[triple, 2 + slot]
        for q in range(qcount):
            lane = (slot * qcount + q) * 2 * LANES
            chosen[triple, :, lane : lane + 2 * LANES] = jnp.where(
                transfer == q, value, jnp.zeros_like(value)
            )

    for triple in range(triples):
        choose(0, triple)
        choose(1, triple)
    tau_all = tau_part[...].reshape(triples * slot_rows, 2 * virtuals)
    wide = qcount * 2 * LANES
    products = lax.dot_general(
        tau_all,
        chosen[...].reshape(triples * slot_rows, 2 * wide),
        (((0,), (0,)), ((), ())),
        preferred_element_type=jnp.float32,
    )
    total = products[:, :wide] + products[:, wide:]
    owned = virtuals // groups
    pieces = []
    for q in range(qcount):
        lane = q * 2 * LANES
        real_lambda = total[:, lane : lane + LANES]
        imag_lambda = total[:, lane + LANES : lane + 2 * LANES]
        pieces.append(real_lambda[:virtuals] + imag_lambda[virtuals:])
        pieces.append(real_lambda[virtuals:] - imag_lambda[:virtuals])
    largest = jnp.abs(pieces[0])
    for piece in pieces[1:]:
        largest = jnp.maximum(largest, jnp.abs(piece))
    largest = jnp.max(jnp.max(largest, 0, keepdims=True), 1, keepdims=True)
    exponent = jnp.floor(jnp.log2(jnp.maximum(largest, SMALLEST)))
    scale = jnp.exp2(HEADROOM - exponent)
    note = jnp.broadcast_to(exponent, (SUBLANES - owned, LANES))
    for number, piece in enumerate(pieces):
        scaled = piece * scale
        for place, group in enumerate(ring):
            out_ref[place, number * SUBLANES : (number + 1) * SUBLANES] = jnp.concatenate(
                [scaled[group * owned : (group + 1) * owned], note], 0
            ).astype(out_ref.dtype)


def pair_terms(slots, packed, virtuals, ring):
    groups, depth, width = packed.shape
    slot_rows = -(-depth // 16) * 16
    triples = 2 * groups
    return pl.pallas_call(
        lambda *refs: pair_kernel(virtuals, ring, *refs),
        out_shape=jax.ShapeDtypeStruct((groups, 4 * SUBLANES, LANES), jnp.float32),
        in_specs=[pl.BlockSpec(memory_space=pl.ANY), pl.BlockSpec(memory_space=pltpu.VMEM)],
        out_specs=pl.BlockSpec(memory_space=pltpu.VMEM),
        scratch_shapes=[
            pltpu.VMEM((triples, slot_rows, 2 * virtuals), jnp.bfloat16),
            pltpu.VMEM((triples, slot_rows, 2 * LANES), jnp.bfloat16),
            pltpu.VMEM((triples, slot_rows, 8 * LANES), jnp.bfloat16),
            pltpu.SMEM(slots.shape, jnp.int32),
            pltpu.SemaphoreType.DMA,
        ],
        compiler_params=pltpu.CompilerParams(vmem_limit_bytes=40 * 2**20),
        name="pairs",
    )(slots, packed)


def factor_kernel(far, parts_ref, factors_ref, out_ref):
    qcount, depth, _ = factors_ref.shape
    owned = out_ref.shape[1]
    virtuals = depth // 2
    for q in range(qcount):
        density = []
        for component in range(2):
            total = parts_ref[q * far * 2 + component].astype(jnp.float32)
            for step in range(1, far):
                total += parts_ref[(q * far + step) * 2 + component].astype(jnp.float32)
            density.append(total[:, :virtuals])
        real, imag = density
        upper = jnp.concatenate([real, -imag], 1)
        lower = jnp.concatenate([imag, real], 1)
        rows = jnp.concatenate([upper, lower], 0)
        high = rows.astype(jnp.bfloat16)
        low = (rows - high.astype(jnp.float32)).astype(jnp.bfloat16)
        both = jnp.concatenate([high, low], 0)
        gamma = jnp.dot(both, factors_ref[q], preferred_element_type=jnp.float32)
        gamma = gamma[: 2 * SUBLANES] + gamma[2 * SUBLANES :]
        for row in range(owned):
            out_ref[q, row] = jnp.concatenate(
                [gamma[row : row + 1], gamma[SUBLANES + row : SUBLANES + row + 1]], 0
            )


def factor_product(parts, factors, owned, far):
    qcount, _, columns = factors.shape
    return pl.pallas_call(
        lambda *refs: factor_kernel(far, *refs),
        out_shape=jax.ShapeDtypeStruct((qcount, owned, 2, columns), jnp.float32),
        in_specs=[pl.BlockSpec(memory_space=pltpu.VMEM)] * 2,
        out_specs=pl.BlockSpec(memory_space=pltpu.VMEM),
        compiler_params=pltpu.CompilerParams(vmem_limit_bytes=24 * 2**20),
        name="factors",
    )(parts, factors)


def local(tau_slabs, lambda_slabs, aux_factor, transfer_table):
    groups = lax.axis_size("kring")
    virtuals = tau_slabs.shape[2]
    contracted = tau_slabs.shape[3]
    qcount = aux_factor.shape[0]
    rows = tau_slabs.shape[0] * 2 * virtuals
    owned = virtuals // groups
    packed, slots = pack(
        tau_slabs.reshape(rows, contracted), lambda_slabs.reshape(rows, contracted), transfer_table
    )
    packed = packed.reshape(groups, contracted // groups, 2 * rows)
    start = groups - groups // 4
    ring = [group ^ 1 for group in [*range(start, groups), *range(start)]]
    exchanged = lax.all_to_all(packed, "kring", 0, 0, axis_index_groups=[ring])
    partial = pair_terms(slots, exchanged, virtuals, ring)
    near = ("kring", "y_lo", "z_lo")
    orb = ("y_lo", "z_hi", "z_lo")
    pieces = lax.axis_size(near) // groups
    members = [[group * pieces + piece for group in ring for piece in range(pieces)]]
    tiles = partial.reshape(lax.axis_size(near), SUBLANES, LANES).astype(jnp.float16)
    tiles = lax.all_to_all(tiles, near, 0, 0, axis_index_groups=members).astype(jnp.float32)
    tile = (tiles * jnp.exp2(tiles[:, owned : owned + 1, :] - HEADROOM)).sum(0)
    tile = tile.astype(jnp.bfloat16)
    copies = jnp.broadcast_to(tile[None], (lax.axis_size(orb),) + tile.shape)
    half = lax.axis_size(orb) // 4
    order = [[*range(half, 2 * half), *range(half), *range(2 * half, 4 * half)]]
    parts = lax.all_to_all(copies, orb, 0, 0, axis_index_groups=order)
    factors = aux_factor.reshape(qcount, 2 * virtuals, aux_factor.shape[3])
    gamma = factor_product(parts, factors, owned, lax.axis_size("z_hi"))
    return gamma.transpose(0, 2, 1, 3)


def solution(mesh):
    groups, spread = mesh.devices.shape
    parts = jax.sharding.Mesh(
        mesh.devices.reshape(groups, 2, spread // 4, 2), ("kring", "y_lo", "z_hi", "z_lo")
    )
    orb = ("y_lo", "z_hi", "z_lo")
    in_specs = (
        P("kring", None, None, orb),
        P("kring", None, None, orb),
        P(None, None, None, orb),
        P(),
    )
    out_specs = P(None, None, "kring", orb)
    return jax.shard_map(local, mesh=parts, in_specs=in_specs, out_specs=out_specs, check_vma=False)
```

```python
import jax
import jax.numpy as jnp
from jax import lax
from jax.experimental import pallas as pl
from jax.experimental.pallas import tpu as pltpu
from jax.sharding import PartitionSpec as P

LANES = 128
SUBLANES = 8
SMALLEST = 2.0**-100
HEADROOM = 13.0
SUM_HEADROOM = 7.0


def partner_slots(table, shape):
    none = 2
    column = lax.broadcasted_iota(jnp.int32, table.shape, 1)
    used = table != none
    first = jnp.min(jnp.where(used, column, table.shape[1] - 1), 1, keepdims=True)
    last = jnp.max(jnp.where(used, column, 0), 1, keepdims=True)
    first_q = jnp.sum(jnp.where(column == first, table, 0), 1, keepdims=True)
    last_q = jnp.sum(jnp.where(column == last, table, 0), 1, keepdims=True)
    last_q = jnp.where(last == first, none, last_q)
    place = lax.broadcasted_iota(jnp.int32, shape, 1)
    return jnp.where(
        place == 0, first, jnp.where(place == 1, last, jnp.where(place == 2, first_q, last_q))
    )


def pack_kernel(
    tau_ref, lambda_ref, table_ref, packed_ref, slots_ref, both, turned, table_here, slots_here, arrived, left
):
    rows, contracted = tau_ref.shape
    tiles = contracted // LANES
    table_copy = pltpu.make_async_copy(table_ref, table_here, arrived.at[2 * tiles])
    table_copy.start()
    incoming = []
    for tile in range(tiles):
        lanes = pl.ds(tile * LANES, LANES)
        for part, source in enumerate((tau_ref, lambda_ref)):
            incoming.append(
                pltpu.make_async_copy(
                    source.at[:, lanes],
                    both.at[tile, pl.ds(part * rows, rows)],
                    arrived.at[2 * tile + part],
                )
            )
    for copy in incoming:
        copy.start()
    table_copy.wait()
    slots_here[...] = partner_slots(table_here[...], slots_here.shape)
    slots_copy = pltpu.make_async_copy(slots_here, slots_ref, left.at[tiles])
    slots_copy.start()
    outgoing = [slots_copy]
    for tile in range(tiles):
        incoming[2 * tile].wait()
        incoming[2 * tile + 1].wait()
        turned[tile] = both[tile].T
        copy = pltpu.make_async_copy(
            turned.at[tile], packed_ref.at[pl.ds(tile * LANES, LANES)], left.at[tile]
        )
        copy.start()
        outgoing.append(copy)
    for copy in outgoing:
        copy.wait()


def pack(tau_rows, lambda_rows, table):
    rows, contracted = tau_rows.shape
    tiles = contracted // LANES
    return pl.pallas_call(
        pack_kernel,
        out_shape=(
            jax.ShapeDtypeStruct((contracted, 2 * rows), jnp.bfloat16),
            jax.ShapeDtypeStruct((table.shape[0], LANES), jnp.int32),
        ),
        in_specs=[pl.BlockSpec(memory_space=pltpu.HBM)] * 3,
        out_specs=(pl.BlockSpec(memory_space=pltpu.HBM),) * 2,
        scratch_shapes=[
            pltpu.VMEM((tiles, 2 * rows, LANES), jnp.bfloat16),
            pltpu.VMEM((tiles, LANES, 2 * rows), jnp.bfloat16),
            pltpu.VMEM(table.shape, jnp.int32),
            pltpu.VMEM((table.shape[0], LANES), jnp.int32),
            pltpu.SemaphoreType.DMA((2 * tiles + 1,)),
            pltpu.SemaphoreType.DMA((tiles + 1,)),
        ],
        compiler_params=pltpu.CompilerParams(vmem_limit_bytes=56 * 2**20),
        name="pack",
    )(tau_rows, lambda_rows, table)


def pair_kernel(
    virtuals, ring, slots_ref, packed_ref, out_ref, tau_part, lambda_part, chosen, slots, arrived
):
    slots_copy = pltpu.make_async_copy(slots_ref, slots, arrived)
    slots_copy.start()
    groups, depth, width = packed_ref.shape
    triples = 2 * groups
    slot_rows = tau_part.shape[1]
    qcount = 2
    half = width // 2
    fill = jnp.zeros((slot_rows - depth, half), jnp.float32)
    lane_fill = jnp.zeros((slot_rows, LANES - virtuals), jnp.bfloat16)
    for place, group in enumerate(ring):
        block = packed_ref[place].astype(jnp.float32)
        tau_block = jnp.concatenate([block[:, :half], fill], 0).astype(jnp.bfloat16)
        lambda_block = jnp.concatenate([block[:, half:], fill], 0).astype(jnp.bfloat16)
        for local_triple in range(2):
            start = local_triple * 2 * virtuals
            tau_part[2 * group + local_triple] = tau_block[:, start : start + 2 * virtuals]
            lambda_part[2 * group + local_triple] = jnp.concatenate(
                [
                    lambda_block[:, start : start + virtuals],
                    lane_fill,
                    lambda_block[:, start + virtuals : start + 2 * virtuals],
                    lane_fill,
                ],
                1,
            )

    slots_copy.wait()

    def choose(slot, triple):
        value = lambda_part[slots[triple, slot]]
        transfer = slots[triple, 2 + slot]
        for q in range(qcount):
            lane = (slot * qcount + q) * 2 * LANES
            chosen[triple, :, lane : lane + 2 * LANES] = jnp.where(
                transfer == q, value, jnp.zeros_like(value)
            )

    for triple in range(triples):
        choose(0, triple)
        choose(1, triple)
    tau_all = tau_part[...].reshape(triples * slot_rows, 2 * virtuals)
    wide = qcount * 2 * LANES
    products = lax.dot_general(
        tau_all,
        chosen[...].reshape(triples * slot_rows, 2 * wide),
        (((0,), (0,)), ((), ())),
        preferred_element_type=jnp.float32,
    )
    total = products[:, :wide] + products[:, wide:]
    owned = virtuals // groups
    pieces = []
    for q in range(qcount):
        lane = q * 2 * LANES
        real_lambda = total[:, lane : lane + LANES]
        imag_lambda = total[:, lane + LANES : lane + 2 * LANES]
        pieces.append(real_lambda[:virtuals] + imag_lambda[virtuals:])
        pieces.append(real_lambda[virtuals:] - imag_lambda[:virtuals])
    largest = jnp.abs(pieces[0])
    for piece in pieces[1:]:
        largest = jnp.maximum(largest, jnp.abs(piece))
    largest = jnp.max(jnp.max(largest, 0, keepdims=True), 1, keepdims=True)
    exponent = jnp.floor(jnp.log2(jnp.maximum(largest, SMALLEST)))
    scale = jnp.exp2(HEADROOM - exponent)
    note = jnp.broadcast_to(exponent, (SUBLANES - owned, LANES))
    for number, piece in enumerate(pieces):
        scaled = piece * scale
        for place, group in enumerate(ring):
            out_ref[place, number * SUBLANES : (number + 1) * SUBLANES] = jnp.concatenate(
                [scaled[group * owned : (group + 1) * owned], note], 0
            ).astype(out_ref.dtype)


def pair_terms(slots, packed, virtuals, ring):
    groups, depth, width = packed.shape
    slot_rows = -(-depth // 16) * 16
    triples = 2 * groups
    return pl.pallas_call(
        lambda *refs: pair_kernel(virtuals, ring, *refs),
        out_shape=jax.ShapeDtypeStruct((groups, 4 * SUBLANES, LANES), jnp.float32),
        in_specs=[pl.BlockSpec(memory_space=pl.ANY), pl.BlockSpec(memory_space=pltpu.VMEM)],
        out_specs=pl.BlockSpec(memory_space=pltpu.VMEM),
        scratch_shapes=[
            pltpu.VMEM((triples, slot_rows, 2 * virtuals), jnp.bfloat16),
            pltpu.VMEM((triples, slot_rows, 2 * LANES), jnp.bfloat16),
            pltpu.VMEM((triples, slot_rows, 8 * LANES), jnp.bfloat16),
            pltpu.SMEM(slots.shape, jnp.int32),
            pltpu.SemaphoreType.DMA,
        ],
        compiler_params=pltpu.CompilerParams(vmem_limit_bytes=40 * 2**20),
        name="pairs",
    )(slots, packed)


def factor_kernel(far, parts_ref, factors_ref, out_ref, held, left):
    qcount, depth, _ = factors_ref.shape
    owned = out_ref.shape[1]
    virtuals = depth // 2

    def unscaled(at):
        part = parts_ref[at]
        return part * jnp.exp2(part[owned : owned + 1] - SUM_HEADROOM)

    outgoing = []
    for q in range(qcount):
        density = []
        for component in range(2):
            total = unscaled(q * far * 2 + component)
            for step in range(1, far):
                total += unscaled((q * far + step) * 2 + component)
            density.append(total[:, :virtuals].astype(jnp.bfloat16).astype(jnp.float32))
        real, imag = density
        upper = jnp.concatenate([real, -imag], 1)
        lower = jnp.concatenate([imag, real], 1)
        rows = jnp.concatenate([upper, lower], 0).astype(jnp.bfloat16)
        gamma = jnp.dot(rows, factors_ref[q], preferred_element_type=jnp.float32)
        for row in range(owned):
            held[q, row] = jnp.concatenate(
                [gamma[row : row + 1], gamma[SUBLANES + row : SUBLANES + row + 1]], 0
            )
        copy = pltpu.make_async_copy(held.at[q], out_ref.at[q], left.at[q])
        copy.start()
        outgoing.append(copy)
    for copy in outgoing:
        copy.wait()


def factor_product(parts, factors, owned, far):
    qcount, _, columns = factors.shape
    shape = (qcount, owned, 2, columns)
    return pl.pallas_call(
        lambda *refs: factor_kernel(far, *refs),
        out_shape=jax.ShapeDtypeStruct(shape, jnp.float32),
        in_specs=[pl.BlockSpec(memory_space=pltpu.VMEM)] * 2,
        out_specs=pl.BlockSpec(memory_space=pltpu.HBM),
        scratch_shapes=[pltpu.VMEM(shape, jnp.float32), pltpu.SemaphoreType.DMA((qcount,))],
        compiler_params=pltpu.CompilerParams(vmem_limit_bytes=24 * 2**20),
        name="factors",
    )(parts, factors)


def local(tau_slabs, lambda_slabs, aux_factor, transfer_table):
    groups = lax.axis_size("kring")
    virtuals = tau_slabs.shape[2]
    contracted = tau_slabs.shape[3]
    qcount = aux_factor.shape[0]
    rows = tau_slabs.shape[0] * 2 * virtuals
    owned = virtuals // groups
    packed, slots = pack(
        tau_slabs.reshape(rows, contracted), lambda_slabs.reshape(rows, contracted), transfer_table
    )
    packed = packed.reshape(groups, contracted // groups, 2 * rows)
    start = groups - groups // 4
    ring = [group ^ 1 for group in [*range(start, groups), *range(start)]]
    exchanged = lax.all_to_all(packed, "kring", 0, 0, axis_index_groups=[ring])
    partial = pair_terms(slots, exchanged, virtuals, ring)
    near = ("kring", "y_lo", "z_lo")
    orb = ("y_lo", "z_hi", "z_lo")
    pieces = lax.axis_size(near) // groups
    members = [[group * pieces + piece for group in ring for piece in range(pieces)]]
    tiles = partial.reshape(lax.axis_size(near), SUBLANES, LANES).astype(jnp.float16)
    tiles = lax.all_to_all(tiles, near, 0, 0, axis_index_groups=members).astype(jnp.float32)
    exponents = tiles[:, owned : owned + 1, :]
    largest = exponents.max(0)
    tile = (tiles * jnp.exp2(exponents - HEADROOM)).sum(0) * jnp.exp2(SUM_HEADROOM - largest)
    row = lax.broadcasted_iota(jnp.int32, tile.shape, 0)
    tile = jnp.where(row < owned, tile, largest).astype(jnp.float16)
    copies = jnp.broadcast_to(tile[None], (lax.axis_size(orb),) + tile.shape)
    half = lax.axis_size(orb) // 4
    order = [[*range(half, 2 * half), *range(half), *range(2 * half, 4 * half)]]
    parts = lax.all_to_all(copies, orb, 0, 0, axis_index_groups=order).astype(jnp.float32)
    factors = aux_factor.reshape(qcount, 2 * virtuals, aux_factor.shape[3])
    gamma = factor_product(parts, factors, owned, lax.axis_size("z_hi"))
    return gamma.transpose(0, 2, 1, 3)


def solution(mesh):
    groups, spread = mesh.devices.shape
    parts = jax.sharding.Mesh(
        mesh.devices.reshape(groups, 2, spread // 4, 2), ("kring", "y_lo", "z_hi", "z_lo")
    )
    orb = ("y_lo", "z_hi", "z_lo")
    in_specs = (
        P("kring", None, None, orb),
        P("kring", None, None, orb),
        P(None, None, None, orb),
        P(),
    )
    out_specs = P(None, None, "kring", orb)
    return jax.shard_map(local, mesh=parts, in_specs=in_specs, out_specs=out_specs, check_vma=False)
```

```python
import jax
import jax.numpy as jnp
from jax import lax
from jax.experimental import pallas as pl
from jax.experimental.pallas import tpu as pltpu
from jax.sharding import PartitionSpec as P

LANES = 128
SUBLANES = 8
SMALLEST = 2.0**-100
HEADROOM = 13.0


def partner_slots(table, shape):
    none = 2
    column = lax.broadcasted_iota(jnp.int32, table.shape, 1)
    used = table != none
    first = jnp.min(jnp.where(used, column, table.shape[1] - 1), 1, keepdims=True)
    last = jnp.max(jnp.where(used, column, 0), 1, keepdims=True)
    first_q = jnp.sum(jnp.where(column == first, table, 0), 1, keepdims=True)
    last_q = jnp.sum(jnp.where(column == last, table, 0), 1, keepdims=True)
    last_q = jnp.where(last == first, none, last_q)
    place = lax.broadcasted_iota(jnp.int32, shape, 1)
    return jnp.where(
        place == 0, first, jnp.where(place == 1, last, jnp.where(place == 2, first_q, last_q))
    )


def pack_kernel(first, count, tau_ref, lambda_ref, *refs):
    if len(refs) == 5:
        packed_ref, both, turned, arrived, left = refs
    else:
        table_ref, packed_ref, slots_ref, both, turned, arrived, left, table_here, slots_here = refs
    rows = tau_ref.shape[0]
    outgoing = []
    if len(refs) > 5:
        table_copy = pltpu.make_async_copy(table_ref, table_here, arrived.at[2 * count])
        table_copy.start()
    incoming = []
    for tile in range(count):
        lanes = pl.ds((first + tile) * LANES, LANES)
        for part, source in enumerate((tau_ref, lambda_ref)):
            incoming.append(
                pltpu.make_async_copy(
                    source.at[:, lanes],
                    both.at[tile, pl.ds(part * rows, rows)],
                    arrived.at[2 * tile + part],
                )
            )
    for copy in incoming:
        copy.start()
    if len(refs) > 5:
        table_copy.wait()
        slots_here[...] = partner_slots(table_here[...], slots_here.shape)
        slots_copy = pltpu.make_async_copy(slots_here, slots_ref, left.at[count])
        slots_copy.start()
        outgoing.append(slots_copy)
    for tile in range(count):
        incoming[2 * tile].wait()
        incoming[2 * tile + 1].wait()
        turned[tile] = both[tile].T
        copy = pltpu.make_async_copy(
            turned.at[tile], packed_ref.at[pl.ds(tile * LANES, LANES)], left.at[tile]
        )
        copy.start()
        outgoing.append(copy)
    for copy in outgoing:
        copy.wait()


def pack(tau_rows, lambda_rows, first, count, table=None):
    rows = tau_rows.shape[0]
    out_shape = [jax.ShapeDtypeStruct((count * LANES, 2 * rows), jnp.bfloat16)]
    scratch = [
        pltpu.VMEM((count, 2 * rows, LANES), jnp.bfloat16),
        pltpu.VMEM((count, LANES, 2 * rows), jnp.bfloat16),
        pltpu.SemaphoreType.DMA((2 * count + 1,)),
        pltpu.SemaphoreType.DMA((count + 1,)),
    ]
    operands = [tau_rows, lambda_rows]
    if table is not None:
        operands.append(table)
        out_shape.append(jax.ShapeDtypeStruct((table.shape[0], LANES), jnp.int32))
        scratch.append(pltpu.VMEM(table.shape, jnp.int32))
        scratch.append(pltpu.VMEM((table.shape[0], LANES), jnp.int32))
    hbm = pl.BlockSpec(memory_space=pltpu.HBM)
    return pl.pallas_call(
        lambda *refs: pack_kernel(first, count, *refs),
        out_shape=out_shape,
        in_specs=[hbm] * len(operands),
        out_specs=[hbm] * len(out_shape),
        scratch_shapes=scratch,
        compiler_params=pltpu.CompilerParams(vmem_limit_bytes=56 * 2**20),
        cost_estimate=pl.CostEstimate(
            flops=0, bytes_accessed=8 * rows * count * LANES, transcendentals=0
        ),
        name="pack",
    )(*operands)


def pair_pieces(virtuals, ring, slots_ref, packed_ref, tau_part, lambda_part, chosen, slots, arrived):
    slots_copy = pltpu.make_async_copy(slots_ref, slots, arrived)
    slots_copy.start()
    groups, depth, width = packed_ref.shape
    triples = 2 * groups
    slot_rows = tau_part.shape[1]
    qcount = 2
    half = width // 2
    lane_fill = jnp.zeros((slot_rows, LANES - virtuals), jnp.bfloat16)
    for place, group in enumerate(ring):
        block = packed_ref[place]
        if slot_rows > depth:
            fill = jnp.zeros((slot_rows - depth, width), jnp.float32)
            block = jnp.concatenate([block.astype(jnp.float32), fill], 0).astype(jnp.bfloat16)
        for local_triple in range(2):
            start = local_triple * 2 * virtuals
            tau_part[2 * group + local_triple] = block[:, start : start + 2 * virtuals]
            start += half
            lambda_part[2 * group + local_triple] = jnp.concatenate(
                [
                    block[:, start : start + virtuals],
                    lane_fill,
                    block[:, start + virtuals : start + 2 * virtuals],
                    lane_fill,
                ],
                1,
            )
    slots_copy.wait()
    for triple in range(triples):
        for slot in range(2):
            value = lambda_part[slots[triple, slot]]
            transfer = slots[triple, 2 + slot]
            for q in range(qcount):
                lane = (slot * qcount + q) * 2 * LANES
                chosen[triple, :, lane : lane + 2 * LANES] = jnp.where(
                    transfer == q, value, jnp.zeros_like(value)
                )
    wide = qcount * 2 * LANES
    products = lax.dot_general(
        tau_part[...].reshape(triples * slot_rows, 2 * virtuals),
        chosen[...].reshape(triples * slot_rows, 2 * wide),
        (((0,), (0,)), ((), ())),
        preferred_element_type=jnp.float32,
    )
    total = products[:, :wide] + products[:, wide:]
    pieces = []
    for q in range(qcount):
        lane = q * 2 * LANES
        real_lambda = total[:, lane : lane + LANES]
        imag_lambda = total[:, lane + LANES : lane + 2 * LANES]
        pieces.append(real_lambda[:virtuals] + imag_lambda[virtuals:])
        pieces.append(real_lambda[virtuals:] - imag_lambda[:virtuals])
    return pieces


def early_kernel(virtuals, ring, slots_ref, packed_ref, out_ref, *scratch):
    pieces = pair_pieces(virtuals, ring, slots_ref, packed_ref, *scratch)
    for number, piece in enumerate(pieces):
        out_ref[number] = piece


def late_kernel(virtuals, ring, slots_ref, packed_ref, early_ref, out_ref, *scratch):
    groups = packed_ref.shape[0]
    pieces = pair_pieces(virtuals, ring, slots_ref, packed_ref, *scratch)
    pieces = [piece + early_ref[number] for number, piece in enumerate(pieces)]
    owned = virtuals // groups
    largest = jnp.abs(pieces[0])
    for piece in pieces[1:]:
        largest = jnp.maximum(largest, jnp.abs(piece))
    largest = jnp.max(jnp.max(largest, 0, keepdims=True), 1, keepdims=True)
    exponent = jnp.floor(jnp.log2(jnp.maximum(largest, SMALLEST)))
    scale = jnp.exp2(HEADROOM - exponent)
    note = jnp.broadcast_to(exponent, (SUBLANES - owned, LANES))
    for number, piece in enumerate(pieces):
        scaled = piece * scale
        for place, group in enumerate(ring):
            out_ref[place, number * SUBLANES : (number + 1) * SUBLANES] = jnp.concatenate(
                [scaled[group * owned : (group + 1) * owned], note], 0
            ).astype(out_ref.dtype)


def pair_terms(slots, packed, virtuals, ring, early=None):
    groups, depth, width = packed.shape
    slot_rows = -(-depth // 16) * 16
    triples = 2 * groups
    vmem = pl.BlockSpec(memory_space=pltpu.VMEM)
    operands = [slots, packed]
    if early is None:
        kernel = early_kernel
        shape = (4, virtuals, LANES)
    else:
        operands.append(early)
        kernel = late_kernel
        shape = (groups, 4 * SUBLANES, LANES)
    return pl.pallas_call(
        lambda *refs: kernel(virtuals, ring, *refs),
        out_shape=jax.ShapeDtypeStruct(shape, jnp.float32),
        in_specs=[pl.BlockSpec(memory_space=pl.ANY)] + [vmem] * (len(operands) - 1),
        out_specs=vmem,
        scratch_shapes=[
            pltpu.VMEM((triples, slot_rows, 2 * virtuals), jnp.bfloat16),
            pltpu.VMEM((triples, slot_rows, 2 * LANES), jnp.bfloat16),
            pltpu.VMEM((triples, slot_rows, 8 * LANES), jnp.bfloat16),
            pltpu.SMEM(slots.shape, jnp.int32),
            pltpu.SemaphoreType.DMA,
        ],
        compiler_params=pltpu.CompilerParams(vmem_limit_bytes=40 * 2**20),
        cost_estimate=pl.CostEstimate(
            flops=32 * triples * slot_rows * virtuals * LANES,
            bytes_accessed=2 * groups * depth * width,
            transcendentals=0,
        ),
        name="pairs",
    )(*operands)


def factor_kernel(far, parts_ref, factors_ref, out_ref):
    qcount, depth, _ = factors_ref.shape
    owned = out_ref.shape[1]
    virtuals = depth // 2
    for q in range(qcount):
        density = []
        for component in range(2):
            total = parts_ref[q * far * 2 + component].astype(jnp.float32)
            for step in range(1, far):
                total += parts_ref[(q * far + step) * 2 + component].astype(jnp.float32)
            density.append(total[:, :virtuals])
        real, imag = density
        upper = jnp.concatenate([real, -imag], 1)
        lower = jnp.concatenate([imag, real], 1)
        rows = jnp.concatenate([upper, lower], 0)
        high = rows.astype(jnp.bfloat16)
        low = (rows - high.astype(jnp.float32)).astype(jnp.bfloat16)
        both = jnp.concatenate([high, low], 0)
        gamma = jnp.dot(both, factors_ref[q], preferred_element_type=jnp.float32)
        gamma = gamma[: 2 * SUBLANES] + gamma[2 * SUBLANES :]
        for row in range(owned):
            out_ref[q, row] = jnp.concatenate(
                [gamma[row : row + 1], gamma[SUBLANES + row : SUBLANES + row + 1]], 0
            )


def factor_product(parts, factors, owned, far):
    qcount, _, columns = factors.shape
    return pl.pallas_call(
        lambda *refs: factor_kernel(far, *refs),
        out_shape=jax.ShapeDtypeStruct((qcount, owned, 2, columns), jnp.float32),
        in_specs=[pl.BlockSpec(memory_space=pltpu.VMEM)] * 2,
        out_specs=pl.BlockSpec(memory_space=pltpu.VMEM),
        compiler_params=pltpu.CompilerParams(vmem_limit_bytes=24 * 2**20),
        name="factors",
    )(parts, factors)


def local(tau_slabs, lambda_slabs, aux_factor, transfer_table):
    groups = lax.axis_size("kring")
    virtuals = tau_slabs.shape[2]
    contracted = tau_slabs.shape[3]
    qcount = aux_factor.shape[0]
    rows = tau_slabs.shape[0] * 2 * virtuals
    owned = virtuals // groups
    tau_rows = tau_slabs.reshape(rows, contracted)
    lambda_rows = lambda_slabs.reshape(rows, contracted)
    tiles = contracted // LANES
    split = -(-tiles // 2)
    start = groups - groups // 4
    ring = [group ^ 1 for group in [*range(start, groups), *range(start)]]

    def exchanged(packed):
        packed = packed.reshape(groups, packed.shape[0] // groups, 2 * rows)
        return lax.all_to_all(packed, "kring", 0, 0, axis_index_groups=[ring])

    packed, slots = pack(tau_rows, lambda_rows, 0, split, transfer_table)
    first = exchanged(packed)
    (packed,) = pack(tau_rows, lambda_rows, split, tiles - split)
    second = exchanged(packed)
    early = pair_terms(slots, first, virtuals, ring)
    partial = pair_terms(slots, second, virtuals, ring, early)
    near = ("kring", "y_lo", "z_lo")
    orb = ("y_lo", "z_hi", "z_lo")
    pieces = lax.axis_size(near) // groups
    members = [[group * pieces + piece for group in ring for piece in range(pieces)]]
    tiles = partial.reshape(lax.axis_size(near), SUBLANES, LANES).astype(jnp.float16)
    tiles = lax.all_to_all(tiles, near, 0, 0, axis_index_groups=members).astype(jnp.float32)
    tile = (tiles * jnp.exp2(tiles[:, owned : owned + 1, :] - HEADROOM)).sum(0)
    tile = tile.astype(jnp.bfloat16)
    copies = jnp.broadcast_to(tile[None], (lax.axis_size(orb),) + tile.shape)
    half = lax.axis_size(orb) // 4
    order = [[*range(half, 2 * half), *range(half), *range(2 * half, 4 * half)]]
    parts = lax.all_to_all(copies, orb, 0, 0, axis_index_groups=order)
    factors = aux_factor.reshape(qcount, 2 * virtuals, aux_factor.shape[3])
    gamma = factor_product(parts, factors, owned, lax.axis_size("z_hi"))
    return gamma.transpose(0, 2, 1, 3)


def solution(mesh):
    groups, spread = mesh.devices.shape
    parts = jax.sharding.Mesh(
        mesh.devices.reshape(groups, 2, spread // 4, 2), ("kring", "y_lo", "z_hi", "z_lo")
    )
    orb = ("y_lo", "z_hi", "z_lo")
    in_specs = (
        P("kring", None, None, orb),
        P("kring", None, None, orb),
        P(None, None, None, orb),
        P(),
    )
    out_specs = P(None, None, "kring", orb)
    return jax.shard_map(local, mesh=parts, in_specs=in_specs, out_specs=out_specs, check_vma=False)
```

```python
import jax
import jax.numpy as jnp
from jax import lax
from jax.experimental import pallas as pl
from jax.experimental.pallas import tpu as pltpu
from jax.sharding import PartitionSpec as P

LANES = 128
SUBLANES = 8
SMALLEST = 2.0**-100
HEADROOM = 13.0
SUM_HEADROOM = 7.0


def partner_slots(table, shape):
    none = 2
    column = lax.broadcasted_iota(jnp.int32, table.shape, 1)
    used = table != none
    first = jnp.min(jnp.where(used, column, table.shape[1] - 1), 1, keepdims=True)
    last = jnp.max(jnp.where(used, column, 0), 1, keepdims=True)
    first_q = jnp.sum(jnp.where(column == first, table, 0), 1, keepdims=True)
    last_q = jnp.sum(jnp.where(column == last, table, 0), 1, keepdims=True)
    last_q = jnp.where(last == first, none, last_q)
    place = lax.broadcasted_iota(jnp.int32, shape, 1)
    return jnp.where(
        place == 0, first, jnp.where(place == 1, last, jnp.where(place == 2, first_q, last_q))
    )


def pack_kernel(
    tau_ref, lambda_ref, table_ref, packed_ref, slots_ref, both, turned, table_here, slots_here, arrived, left
):
    rows, contracted = tau_ref.shape
    tiles = contracted // LANES
    table_copy = pltpu.make_async_copy(table_ref, table_here, arrived.at[2 * tiles])
    table_copy.start()
    incoming = []
    for tile in range(tiles):
        lanes = pl.ds(tile * LANES, LANES)
        for part, source in enumerate((tau_ref, lambda_ref)):
            incoming.append(
                pltpu.make_async_copy(
                    source.at[:, lanes],
                    both.at[tile, pl.ds(part * rows, rows)],
                    arrived.at[2 * tile + part],
                )
            )
    for copy in incoming:
        copy.start()
    table_copy.wait()
    slots_here[...] = partner_slots(table_here[...], slots_here.shape)
    slots_copy = pltpu.make_async_copy(slots_here, slots_ref, left.at[tiles])
    slots_copy.start()
    outgoing = [slots_copy]
    for tile in range(tiles):
        incoming[2 * tile].wait()
        incoming[2 * tile + 1].wait()
        turned[tile] = both[tile].T
        copy = pltpu.make_async_copy(
            turned.at[tile], packed_ref.at[pl.ds(tile * LANES, LANES)], left.at[tile]
        )
        copy.start()
        outgoing.append(copy)
    for copy in outgoing:
        copy.wait()


def pack(tau_rows, lambda_rows, table):
    rows, contracted = tau_rows.shape
    tiles = contracted // LANES
    return pl.pallas_call(
        pack_kernel,
        out_shape=(
            jax.ShapeDtypeStruct((contracted, 2 * rows), jnp.bfloat16),
            jax.ShapeDtypeStruct((table.shape[0], LANES), jnp.int32),
        ),
        in_specs=[pl.BlockSpec(memory_space=pltpu.HBM)] * 3,
        out_specs=(pl.BlockSpec(memory_space=pltpu.HBM),) * 2,
        scratch_shapes=[
            pltpu.VMEM((tiles, 2 * rows, LANES), jnp.bfloat16),
            pltpu.VMEM((tiles, LANES, 2 * rows), jnp.bfloat16),
            pltpu.VMEM(table.shape, jnp.int32),
            pltpu.VMEM((table.shape[0], LANES), jnp.int32),
            pltpu.SemaphoreType.DMA((2 * tiles + 1,)),
            pltpu.SemaphoreType.DMA((tiles + 1,)),
        ],
        compiler_params=pltpu.CompilerParams(vmem_limit_bytes=56 * 2**20),
        name="pack",
    )(tau_rows, lambda_rows, table)


def pair_kernel(
    virtuals, ring, slots_ref, packed_ref, out_ref, tau_part, lambda_part, chosen, slots, arrived
):
    slots_copy = pltpu.make_async_copy(slots_ref, slots, arrived)
    slots_copy.start()
    groups, depth, width = packed_ref.shape
    triples = 2 * groups
    slot_rows = tau_part.shape[1]
    qcount = 2
    half = width // 2
    fill = jnp.zeros((slot_rows - depth, half), jnp.float32)
    lane_fill = jnp.zeros((slot_rows, LANES - virtuals), jnp.bfloat16)
    for place, group in enumerate(ring):
        block = packed_ref[place].astype(jnp.float32)
        tau_block = jnp.concatenate([block[:, :half], fill], 0).astype(jnp.bfloat16)
        lambda_block = jnp.concatenate([block[:, half:], fill], 0).astype(jnp.bfloat16)
        for local_triple in range(2):
            start = local_triple * 2 * virtuals
            tau_part[2 * group + local_triple] = tau_block[:, start : start + 2 * virtuals]
            lambda_part[2 * group + local_triple] = jnp.concatenate(
                [
                    lambda_block[:, start : start + virtuals],
                    lane_fill,
                    lambda_block[:, start + virtuals : start + 2 * virtuals],
                    lane_fill,
                ],
                1,
            )

    slots_copy.wait()

    def choose(slot, triple):
        value = lambda_part[slots[triple, slot]]
        transfer = slots[triple, 2 + slot]
        for q in range(qcount):
            lane = (slot * qcount + q) * 2 * LANES
            chosen[triple, :, lane : lane + 2 * LANES] = jnp.where(
                transfer == q, value, jnp.zeros_like(value)
            )

    for triple in range(triples):
        choose(0, triple)
        choose(1, triple)
    tau_all = tau_part[...].reshape(triples * slot_rows, 2 * virtuals)
    wide = qcount * 2 * LANES
    products = lax.dot_general(
        tau_all,
        chosen[...].reshape(triples * slot_rows, 2 * wide),
        (((0,), (0,)), ((), ())),
        preferred_element_type=jnp.float32,
    )
    total = products[:, :wide] + products[:, wide:]
    owned = virtuals // groups
    pieces = []
    for q in range(qcount):
        lane = q * 2 * LANES
        real_lambda = total[:, lane : lane + LANES]
        imag_lambda = total[:, lane + LANES : lane + 2 * LANES]
        pieces.append(real_lambda[:virtuals] + imag_lambda[virtuals:])
        pieces.append(real_lambda[virtuals:] - imag_lambda[:virtuals])
    largest = jnp.abs(pieces[0])
    for piece in pieces[1:]:
        largest = jnp.maximum(largest, jnp.abs(piece))
    largest = jnp.max(jnp.max(largest, 0, keepdims=True), 1, keepdims=True)
    exponent = jnp.floor(jnp.log2(jnp.maximum(largest, SMALLEST)))
    scale = jnp.exp2(HEADROOM - exponent)
    note = jnp.broadcast_to(exponent, (SUBLANES - owned, LANES))
    for number, piece in enumerate(pieces):
        scaled = piece * scale
        for place, group in enumerate(ring):
            out_ref[place, number * SUBLANES : (number + 1) * SUBLANES] = jnp.concatenate(
                [scaled[group * owned : (group + 1) * owned], note], 0
            ).astype(out_ref.dtype)


def pair_terms(slots, packed, virtuals, ring):
    groups, depth, width = packed.shape
    slot_rows = -(-depth // 16) * 16
    triples = 2 * groups
    return pl.pallas_call(
        lambda *refs: pair_kernel(virtuals, ring, *refs),
        out_shape=jax.ShapeDtypeStruct((groups, 4 * SUBLANES, LANES), jnp.float32),
        in_specs=[pl.BlockSpec(memory_space=pl.ANY), pl.BlockSpec(memory_space=pltpu.VMEM)],
        out_specs=pl.BlockSpec(memory_space=pltpu.VMEM),
        scratch_shapes=[
            pltpu.VMEM((triples, slot_rows, 2 * virtuals), jnp.bfloat16),
            pltpu.VMEM((triples, slot_rows, 2 * LANES), jnp.bfloat16),
            pltpu.VMEM((triples, slot_rows, 8 * LANES), jnp.bfloat16),
            pltpu.SMEM(slots.shape, jnp.int32),
            pltpu.SemaphoreType.DMA,
        ],
        compiler_params=pltpu.CompilerParams(vmem_limit_bytes=40 * 2**20),
        name="pairs",
    )(slots, packed)


def factor_kernel(far, parts_ref, factors_ref, out_ref, held, left):
    qcount, depth, _ = factors_ref.shape
    owned = out_ref.shape[1]
    virtuals = depth // 2

    def unscaled(at):
        part = parts_ref[at]
        return part * jnp.exp2(part[owned : owned + 1] - SUM_HEADROOM)

    outgoing = []
    for q in range(qcount):
        density = []
        for component in range(2):
            total = unscaled(q * far * 2 + component)
            for step in range(1, far):
                total += unscaled((q * far + step) * 2 + component)
            density.append(total[:, :virtuals].astype(jnp.bfloat16).astype(jnp.float32))
        real, imag = density
        upper = jnp.concatenate([real, -imag], 1)
        lower = jnp.concatenate([imag, real], 1)
        rows = jnp.concatenate([upper, lower], 0).astype(jnp.bfloat16)
        gamma = jnp.dot(rows, factors_ref[q], preferred_element_type=jnp.float32)
        for row in range(owned):
            held[q, row] = jnp.concatenate(
                [gamma[row : row + 1], gamma[SUBLANES + row : SUBLANES + row + 1]], 0
            )
        copy = pltpu.make_async_copy(held.at[q], out_ref.at[q], left.at[q])
        copy.start()
        outgoing.append(copy)
    for copy in outgoing:
        copy.wait()


def factor_product(parts, factors, owned, far):
    qcount, _, columns = factors.shape
    shape = (qcount, owned, 2, columns)
    return pl.pallas_call(
        lambda *refs: factor_kernel(far, *refs),
        out_shape=jax.ShapeDtypeStruct(shape, jnp.float32),
        in_specs=[pl.BlockSpec(memory_space=pltpu.VMEM)] * 2,
        out_specs=pl.BlockSpec(memory_space=pltpu.HBM),
        scratch_shapes=[pltpu.VMEM(shape, jnp.float32), pltpu.SemaphoreType.DMA((qcount,))],
        compiler_params=pltpu.CompilerParams(vmem_limit_bytes=24 * 2**20),
        name="factors",
    )(parts, factors)


def local(tau_slabs, lambda_slabs, aux_factor, transfer_table):
    groups = lax.axis_size("kring")
    virtuals = tau_slabs.shape[2]
    contracted = tau_slabs.shape[3]
    qcount = aux_factor.shape[0]
    rows = tau_slabs.shape[0] * 2 * virtuals
    owned = virtuals // groups
    packed, slots = pack(
        tau_slabs.reshape(rows, contracted), lambda_slabs.reshape(rows, contracted), transfer_table
    )
    packed = packed.reshape(groups, contracted // groups, 2 * rows)
    start = groups - groups // 4
    ring = [group ^ 1 for group in [*range(start, groups), *range(start)]]
    exchanged = lax.all_to_all(packed, "kring", 0, 0, axis_index_groups=[ring])
    partial = pair_terms(slots, exchanged, virtuals, ring)
    near = ("kring", "y_lo", "z_lo")
    orb = ("y_lo", "z_hi", "z_lo")
    pieces = lax.axis_size(near) // groups
    members = [[group * pieces + piece for group in ring for piece in range(pieces)]]
    tiles = partial.reshape(lax.axis_size(near), SUBLANES, LANES).astype(jnp.float16)
    tiles = lax.all_to_all(tiles, near, 0, 0, axis_index_groups=members).astype(jnp.float32)
    exponents = tiles[:, owned : owned + 1, :]
    largest = exponents.max(0)
    tile = (tiles * jnp.exp2(exponents - HEADROOM)).sum(0) * jnp.exp2(SUM_HEADROOM - largest)
    tile = jnp.concatenate([tile[:owned], largest], 0).astype(jnp.float16)
    copies = jnp.broadcast_to(tile[None], (lax.axis_size(orb),) + tile.shape)
    half = lax.axis_size(orb) // 4
    order = [[*range(half, 2 * half), *range(half), *range(2 * half, 4 * half)]]
    parts = lax.all_to_all(copies, orb, 0, 0, axis_index_groups=order).astype(jnp.float32)
    factors = aux_factor.reshape(qcount, 2 * virtuals, aux_factor.shape[3])
    gamma = factor_product(parts, factors, owned, lax.axis_size("z_hi"))
    return gamma.transpose(0, 2, 1, 3)


def solution(mesh):
    groups, spread = mesh.devices.shape
    parts = jax.sharding.Mesh(
        mesh.devices.reshape(groups, 2, spread // 4, 2), ("kring", "y_lo", "z_hi", "z_lo")
    )
    orb = ("y_lo", "z_hi", "z_lo")
    in_specs = (
        P("kring", None, None, orb),
        P("kring", None, None, orb),
        P(None, None, None, orb),
        P(),
    )
    out_specs = P(None, None, "kring", orb)
    return jax.shard_map(local, mesh=parts, in_specs=in_specs, out_specs=out_specs, check_vma=False)
```

```python
import jax
import jax.numpy as jnp
from jax import lax
from jax.experimental import pallas as pl
from jax.experimental.pallas import tpu as pltpu
from jax.sharding import PartitionSpec as P

LANES = 128
SUBLANES = 8
SMALLEST = 2.0**-100
HEADROOM = 13.0
SUM_HEADROOM = 7.0


def partner_slots(table, shape):
    none = 2
    column = lax.broadcasted_iota(jnp.int32, table.shape, 1)
    used = table != none
    first = jnp.min(jnp.where(used, column, table.shape[1] - 1), 1, keepdims=True)
    last = jnp.max(jnp.where(used, column, 0), 1, keepdims=True)
    first_q = jnp.sum(jnp.where(column == first, table, 0), 1, keepdims=True)
    last_q = jnp.sum(jnp.where(column == last, table, 0), 1, keepdims=True)
    last_q = jnp.where(last == first, none, last_q)
    place = lax.broadcasted_iota(jnp.int32, shape, 1)
    return jnp.where(
        place == 0, first, jnp.where(place == 1, last, jnp.where(place == 2, first_q, last_q))
    )


def pack_kernel(
    tau_ref, lambda_ref, table_ref, packed_ref, slots_ref, both, table_here, slots_here, arrived, left
):
    rows, contracted = tau_ref.shape
    tiles = contracted // LANES
    table_copy = pltpu.make_async_copy(table_ref, table_here, arrived.at[2 * tiles])
    table_copy.start()
    incoming = []
    for tile in range(tiles):
        lanes = pl.ds(tile * LANES, LANES)
        for part, source in enumerate((tau_ref, lambda_ref)):
            incoming.append(
                pltpu.make_async_copy(
                    source.at[:, lanes],
                    both.at[tile, pl.ds(part * rows, rows)],
                    arrived.at[2 * tile + part],
                )
            )
    for copy in incoming:
        copy.start()
    table_copy.wait()
    slots_here[...] = partner_slots(table_here[...], slots_here.shape)
    slots_copy = pltpu.make_async_copy(slots_here, slots_ref, left)
    slots_copy.start()
    outgoing = [slots_copy]
    for tile in range(tiles):
        incoming[2 * tile].wait()
        incoming[2 * tile + 1].wait()
        packed_ref[tile * LANES : (tile + 1) * LANES] = both[tile].T
    for copy in outgoing:
        copy.wait()


def pack(tau_rows, lambda_rows, table):
    rows, contracted = tau_rows.shape
    tiles = contracted // LANES
    return pl.pallas_call(
        pack_kernel,
        out_shape=(
            jax.ShapeDtypeStruct((contracted, 2 * rows), jnp.bfloat16),
            jax.ShapeDtypeStruct((table.shape[0], LANES), jnp.int32),
        ),
        in_specs=[pl.BlockSpec(memory_space=pltpu.HBM)] * 3,
        out_specs=(pl.BlockSpec(memory_space=pltpu.VMEM), pl.BlockSpec(memory_space=pltpu.HBM)),
        scratch_shapes=[
            pltpu.VMEM((tiles, 2 * rows, LANES), jnp.bfloat16),
            pltpu.VMEM(table.shape, jnp.int32),
            pltpu.VMEM((table.shape[0], LANES), jnp.int32),
            pltpu.SemaphoreType.DMA((2 * tiles + 1,)),
            pltpu.SemaphoreType.DMA,
        ],
        compiler_params=pltpu.CompilerParams(vmem_limit_bytes=16 * 2**20),
        name="pack",
    )(*(pltpu.with_memory_space_constraint(x, pltpu.HBM) for x in (tau_rows, lambda_rows, table)))


def pair_kernel(
    virtuals, ring, slots_ref, packed_ref, out_ref, tau_part, lambda_part, chosen, slots, arrived
):
    slots_copy = pltpu.make_async_copy(slots_ref, slots, arrived)
    slots_copy.start()
    groups, depth, width = packed_ref.shape
    triples = 2 * groups
    slot_rows = tau_part.shape[1]
    qcount = 2
    half = width // 2
    fill = jnp.zeros((slot_rows - depth, half), jnp.float32)
    lane_fill = jnp.zeros((slot_rows, LANES - virtuals), jnp.bfloat16)
    for place, group in enumerate(ring):
        block = packed_ref[place].astype(jnp.float32)
        tau_block = jnp.concatenate([block[:, :half], fill], 0).astype(jnp.bfloat16)
        lambda_block = jnp.concatenate([block[:, half:], fill], 0).astype(jnp.bfloat16)
        for local_triple in range(2):
            start = local_triple * 2 * virtuals
            tau_part[2 * group + local_triple] = tau_block[:, start : start + 2 * virtuals]
            lambda_part[2 * group + local_triple] = jnp.concatenate(
                [
                    lambda_block[:, start : start + virtuals],
                    lane_fill,
                    lambda_block[:, start + virtuals : start + 2 * virtuals],
                    lane_fill,
                ],
                1,
            )

    slots_copy.wait()

    def choose(slot, triple):
        value = lambda_part[slots[triple, slot]]
        transfer = slots[triple, 2 + slot]
        for q in range(qcount):
            lane = (slot * qcount + q) * 2 * LANES
            chosen[triple, :, lane : lane + 2 * LANES] = jnp.where(
                transfer == q, value, jnp.zeros_like(value)
            )

    for triple in range(triples):
        choose(0, triple)
        choose(1, triple)
    tau_all = tau_part[...].reshape(triples * slot_rows, 2 * virtuals)
    wide = qcount * 2 * LANES
    products = lax.dot_general(
        tau_all,
        chosen[...].reshape(triples * slot_rows, 2 * wide),
        (((0,), (0,)), ((), ())),
        preferred_element_type=jnp.float32,
    )
    total = products[:, :wide] + products[:, wide:]
    owned = virtuals // groups
    pieces = []
    for q in range(qcount):
        lane = q * 2 * LANES
        real_lambda = total[:, lane : lane + LANES]
        imag_lambda = total[:, lane + LANES : lane + 2 * LANES]
        pieces.append(real_lambda[:virtuals] + imag_lambda[virtuals:])
        pieces.append(real_lambda[virtuals:] - imag_lambda[:virtuals])
    largest = jnp.abs(pieces[0])
    for piece in pieces[1:]:
        largest = jnp.maximum(largest, jnp.abs(piece))
    largest = jnp.max(jnp.max(largest, 0, keepdims=True), 1, keepdims=True)
    exponent = jnp.floor(jnp.log2(jnp.maximum(largest, SMALLEST)))
    scale = jnp.exp2(HEADROOM - exponent)
    note = jnp.broadcast_to(exponent, (SUBLANES - owned, LANES))
    for number, piece in enumerate(pieces):
        scaled = piece * scale
        for place, group in enumerate(ring):
            out_ref[place, number * SUBLANES : (number + 1) * SUBLANES] = jnp.concatenate(
                [scaled[group * owned : (group + 1) * owned], note], 0
            ).astype(out_ref.dtype)


def pair_terms(slots, packed, virtuals, ring):
    groups, depth, width = packed.shape
    slot_rows = -(-depth // 16) * 16
    triples = 2 * groups
    return pl.pallas_call(
        lambda *refs: pair_kernel(virtuals, ring, *refs),
        out_shape=jax.ShapeDtypeStruct((groups, 4 * SUBLANES, LANES), jnp.float32),
        in_specs=[pl.BlockSpec(memory_space=pl.ANY), pl.BlockSpec(memory_space=pltpu.VMEM)],
        out_specs=pl.BlockSpec(memory_space=pltpu.VMEM),
        scratch_shapes=[
            pltpu.VMEM((triples, slot_rows, 2 * virtuals), jnp.bfloat16),
            pltpu.VMEM((triples, slot_rows, 2 * LANES), jnp.bfloat16),
            pltpu.VMEM((triples, slot_rows, 8 * LANES), jnp.bfloat16),
            pltpu.SMEM(slots.shape, jnp.int32),
            pltpu.SemaphoreType.DMA,
        ],
        compiler_params=pltpu.CompilerParams(vmem_limit_bytes=40 * 2**20),
        name="pairs",
    )(slots, packed)


def factor_kernel(far, parts_ref, factors_ref, out_ref, held, left):
    qcount, depth, _ = factors_ref.shape
    owned = out_ref.shape[1]
    virtuals = depth // 2

    def unscaled(at):
        part = parts_ref[at]
        return part * jnp.exp2(part[owned : owned + 1] - SUM_HEADROOM)

    outgoing = []
    for q in range(qcount):
        density = []
        for component in range(2):
            total = unscaled(q * far * 2 + component)
            for step in range(1, far):
                total += unscaled((q * far + step) * 2 + component)
            density.append(total[:, :virtuals].astype(jnp.bfloat16).astype(jnp.float32))
        real, imag = density
        upper = jnp.concatenate([real, -imag], 1)
        lower = jnp.concatenate([imag, real], 1)
        rows = jnp.concatenate([upper, lower], 0).astype(jnp.bfloat16)
        gamma = jnp.dot(rows, factors_ref[q], preferred_element_type=jnp.float32)
        for row in range(owned):
            held[q, row] = jnp.concatenate(
                [gamma[row : row + 1], gamma[SUBLANES + row : SUBLANES + row + 1]], 0
            )
        copy = pltpu.make_async_copy(held.at[q], out_ref.at[q], left.at[q])
        copy.start()
        outgoing.append(copy)
    for copy in outgoing:
        copy.wait()


def factor_product(parts, factors, owned, far):
    qcount, _, columns = factors.shape
    shape = (qcount, owned, 2, columns)
    return pl.pallas_call(
        lambda *refs: factor_kernel(far, *refs),
        out_shape=jax.ShapeDtypeStruct(shape, jnp.float32),
        in_specs=[pl.BlockSpec(memory_space=pltpu.VMEM)] * 2,
        out_specs=pl.BlockSpec(memory_space=pltpu.HBM),
        scratch_shapes=[pltpu.VMEM(shape, jnp.float32), pltpu.SemaphoreType.DMA((qcount,))],
        compiler_params=pltpu.CompilerParams(vmem_limit_bytes=24 * 2**20),
        name="factors",
    )(parts, factors)


def local(tau_slabs, lambda_slabs, aux_factor, transfer_table):
    groups = lax.axis_size("kring")
    virtuals = tau_slabs.shape[2]
    contracted = tau_slabs.shape[3]
    qcount = aux_factor.shape[0]
    rows = tau_slabs.shape[0] * 2 * virtuals
    owned = virtuals // groups
    packed, slots = pack(
        tau_slabs.reshape(rows, contracted), lambda_slabs.reshape(rows, contracted), transfer_table
    )
    packed = packed.reshape(groups, contracted // groups, 2 * rows)
    start = groups - groups // 4
    ring = [group ^ 1 for group in [*range(start, groups), *range(start)]]
    exchanged = lax.all_to_all(packed, "kring", 0, 0, axis_index_groups=[ring])
    partial = pair_terms(slots, exchanged, virtuals, ring)
    near = ("kring", "y_lo", "z_lo")
    orb = ("y_lo", "z_hi", "z_lo")
    pieces = lax.axis_size(near) // groups
    members = [[group * pieces + piece for group in ring for piece in range(pieces)]]
    tiles = partial.reshape(lax.axis_size(near), SUBLANES, LANES).astype(jnp.float16)
    tiles = lax.all_to_all(tiles, near, 0, 0, axis_index_groups=members).astype(jnp.float32)
    exponents = tiles[:, owned : owned + 1, :]
    largest = exponents.max(0)
    tile = (tiles * jnp.exp2(exponents - HEADROOM)).sum(0) * jnp.exp2(SUM_HEADROOM - largest)
    tile = jnp.concatenate([tile[:owned], largest], 0).astype(jnp.float16)
    copies = jnp.broadcast_to(tile[None], (lax.axis_size(orb),) + tile.shape)
    half = lax.axis_size(orb) // 4
    order = [[*range(half, 2 * half), *range(half), *range(2 * half, 4 * half)]]
    parts = lax.all_to_all(copies, orb, 0, 0, axis_index_groups=order).astype(jnp.float32)
    factors = aux_factor.reshape(qcount, 2 * virtuals, aux_factor.shape[3])
    gamma = factor_product(parts, factors, owned, lax.axis_size("z_hi"))
    return gamma.transpose(0, 2, 1, 3)


def solution(mesh):
    groups, spread = mesh.devices.shape
    parts = jax.sharding.Mesh(
        mesh.devices.reshape(groups, 2, spread // 4, 2), ("kring", "y_lo", "z_hi", "z_lo")
    )
    orb = ("y_lo", "z_hi", "z_lo")
    in_specs = (
        P("kring", None, None, orb),
        P("kring", None, None, orb),
        P(None, None, None, orb),
        P(),
    )
    out_specs = P(None, None, "kring", orb)
    return jax.shard_map(local, mesh=parts, in_specs=in_specs, out_specs=out_specs, check_vma=False)
```

```python
import jax
import jax.numpy as jnp
from jax import lax
from jax.experimental import pallas as pl
from jax.experimental.pallas import tpu as pltpu
from jax.sharding import PartitionSpec as P

LANES = 128
SUBLANES = 8
SMALLEST = 2.0**-100
HEADROOM = 13.0
SUM_HEADROOM = 7.0


def partner_slots(table, shape):
    none = 2
    column = lax.broadcasted_iota(jnp.int32, table.shape, 1)
    used = table != none
    first = jnp.min(jnp.where(used, column, table.shape[1] - 1), 1, keepdims=True)
    last = jnp.max(jnp.where(used, column, 0), 1, keepdims=True)
    first_q = jnp.sum(jnp.where(column == first, table, 0), 1, keepdims=True)
    last_q = jnp.sum(jnp.where(column == last, table, 0), 1, keepdims=True)
    last_q = jnp.where(last == first, none, last_q)
    place = lax.broadcasted_iota(jnp.int32, shape, 1)
    return jnp.where(
        place == 0, first, jnp.where(place == 1, last, jnp.where(place == 2, first_q, last_q))
    )


def pack_kernel(
    tau_ref, lambda_ref, table_ref, packed_ref, slots_ref, both, table_here, arrived
):
    rows, contracted = tau_ref.shape
    tiles = contracted // LANES
    table_copy = pltpu.make_async_copy(table_ref, table_here, arrived.at[2 * tiles])
    table_copy.start()
    incoming = []
    for tile in range(tiles):
        lanes = pl.ds(tile * LANES, LANES)
        for part, source in enumerate((tau_ref, lambda_ref)):
            incoming.append(
                pltpu.make_async_copy(
                    source.at[:, lanes],
                    both.at[tile, pl.ds(part * rows, rows)],
                    arrived.at[2 * tile + part],
                )
            )
    for copy in incoming:
        copy.start()
    table_copy.wait()
    slots_ref[...] = partner_slots(table_here[...], slots_ref.shape)
    for tile in range(tiles):
        incoming[2 * tile].wait()
        incoming[2 * tile + 1].wait()
        packed_ref[tile * LANES : (tile + 1) * LANES] = both[tile].T


def pack(tau_rows, lambda_rows, table):
    rows, contracted = tau_rows.shape
    tiles = contracted // LANES
    return pl.pallas_call(
        pack_kernel,
        out_shape=(
            jax.ShapeDtypeStruct((contracted, 2 * rows), jnp.bfloat16),
            jax.ShapeDtypeStruct((table.shape[0], LANES), jnp.int32),
        ),
        in_specs=[pl.BlockSpec(memory_space=pltpu.HBM)] * 3,
        out_specs=(pl.BlockSpec(memory_space=pltpu.VMEM),) * 2,
        scratch_shapes=[
            pltpu.VMEM((tiles, 2 * rows, LANES), jnp.bfloat16),
            pltpu.VMEM(table.shape, jnp.int32),
            pltpu.SemaphoreType.DMA((2 * tiles + 1,)),
        ],
        compiler_params=pltpu.CompilerParams(vmem_limit_bytes=16 * 2**20),
        name="pack",
    )(*(pltpu.with_memory_space_constraint(x, pltpu.HBM) for x in (tau_rows, lambda_rows, table)))


def pair_kernel(
    virtuals, ring, slots_ref, packed_ref, out_ref, tau_part, lambda_part, chosen, slots, arrived
):
    slots_copy = pltpu.make_async_copy(slots_ref, slots, arrived)
    slots_copy.start()
    groups, depth, width = packed_ref.shape
    triples = 2 * groups
    slot_rows = tau_part.shape[1]
    qcount = 2
    half = width // 2
    fill = jnp.zeros((slot_rows - depth, half), jnp.float32)
    lane_fill = jnp.zeros((slot_rows, LANES - virtuals), jnp.bfloat16)
    for place, group in enumerate(ring):
        block = packed_ref[place].astype(jnp.float32)
        tau_block = jnp.concatenate([block[:, :half], fill], 0).astype(jnp.bfloat16)
        lambda_block = jnp.concatenate([block[:, half:], fill], 0).astype(jnp.bfloat16)
        for local_triple in range(2):
            start = local_triple * 2 * virtuals
            tau_part[2 * group + local_triple] = tau_block[:, start : start + 2 * virtuals]
            lambda_part[2 * group + local_triple] = jnp.concatenate(
                [
                    lambda_block[:, start : start + virtuals],
                    lane_fill,
                    lambda_block[:, start + virtuals : start + 2 * virtuals],
                    lane_fill,
                ],
                1,
            )

    slots_copy.wait()

    def choose(slot, triple):
        value = lambda_part[slots[triple, slot]]
        transfer = slots[triple, 2 + slot]
        for q in range(qcount):
            lane = (slot * qcount + q) * 2 * LANES
            chosen[triple, :, lane : lane + 2 * LANES] = jnp.where(
                transfer == q, value, jnp.zeros_like(value)
            )

    for triple in range(triples):
        choose(0, triple)
        choose(1, triple)
    tau_all = tau_part[...].reshape(triples * slot_rows, 2 * virtuals)
    wide = qcount * 2 * LANES
    products = lax.dot_general(
        tau_all,
        chosen[...].reshape(triples * slot_rows, 2 * wide),
        (((0,), (0,)), ((), ())),
        preferred_element_type=jnp.float32,
    )
    total = products[:, :wide] + products[:, wide:]
    owned = virtuals // groups
    pieces = []
    for q in range(qcount):
        lane = q * 2 * LANES
        real_lambda = total[:, lane : lane + LANES]
        imag_lambda = total[:, lane + LANES : lane + 2 * LANES]
        pieces.append(real_lambda[:virtuals] + imag_lambda[virtuals:])
        pieces.append(real_lambda[virtuals:] - imag_lambda[:virtuals])
    largest = jnp.abs(pieces[0])
    for piece in pieces[1:]:
        largest = jnp.maximum(largest, jnp.abs(piece))
    largest = jnp.max(jnp.max(largest, 0, keepdims=True), 1, keepdims=True)
    exponent = jnp.floor(jnp.log2(jnp.maximum(largest, SMALLEST)))
    scale = jnp.exp2(HEADROOM - exponent)
    note = jnp.broadcast_to(exponent, (SUBLANES - owned, LANES))
    for number, piece in enumerate(pieces):
        scaled = piece * scale
        for place, group in enumerate(ring):
            out_ref[place, number * SUBLANES : (number + 1) * SUBLANES] = jnp.concatenate(
                [scaled[group * owned : (group + 1) * owned], note], 0
            ).astype(out_ref.dtype)


def pair_terms(slots, packed, virtuals, ring):
    groups, depth, width = packed.shape
    slot_rows = -(-depth // 16) * 16
    triples = 2 * groups
    return pl.pallas_call(
        lambda *refs: pair_kernel(virtuals, ring, *refs),
        out_shape=jax.ShapeDtypeStruct((groups, 4 * SUBLANES, LANES), jnp.float32),
        in_specs=[pl.BlockSpec(memory_space=pl.ANY), pl.BlockSpec(memory_space=pltpu.VMEM)],
        out_specs=pl.BlockSpec(memory_space=pltpu.VMEM),
        scratch_shapes=[
            pltpu.VMEM((triples, slot_rows, 2 * virtuals), jnp.bfloat16),
            pltpu.VMEM((triples, slot_rows, 2 * LANES), jnp.bfloat16),
            pltpu.VMEM((triples, slot_rows, 8 * LANES), jnp.bfloat16),
            pltpu.SMEM(slots.shape, jnp.int32),
            pltpu.SemaphoreType.DMA,
        ],
        compiler_params=pltpu.CompilerParams(vmem_limit_bytes=40 * 2**20),
        name="pairs",
    )(slots, packed)


def factor_kernel(far, parts_ref, factors_ref, out_ref, held, left):
    qcount, depth, _ = factors_ref.shape
    owned = out_ref.shape[1]
    virtuals = depth // 2

    def unscaled(at):
        part = parts_ref[at]
        return part * jnp.exp2(part[owned : owned + 1] - SUM_HEADROOM)

    outgoing = []
    for q in range(qcount):
        density = []
        for component in range(2):
            total = unscaled(q * far * 2 + component)
            for step in range(1, far):
                total += unscaled((q * far + step) * 2 + component)
            density.append(total[:, :virtuals].astype(jnp.bfloat16).astype(jnp.float32))
        real, imag = density
        upper = jnp.concatenate([real, -imag], 1)
        lower = jnp.concatenate([imag, real], 1)
        rows = jnp.concatenate([upper, lower], 0).astype(jnp.bfloat16)
        gamma = jnp.dot(rows, factors_ref[q], preferred_element_type=jnp.float32)
        for row in range(owned):
            held[q, row] = jnp.concatenate(
                [gamma[row : row + 1], gamma[SUBLANES + row : SUBLANES + row + 1]], 0
            )
        copy = pltpu.make_async_copy(held.at[q], out_ref.at[q], left.at[q])
        copy.start()
        outgoing.append(copy)
    for copy in outgoing:
        copy.wait()


def factor_product(parts, factors, owned, far):
    qcount, _, columns = factors.shape
    shape = (qcount, owned, 2, columns)
    return pl.pallas_call(
        lambda *refs: factor_kernel(far, *refs),
        out_shape=jax.ShapeDtypeStruct(shape, jnp.float32),
        in_specs=[pl.BlockSpec(memory_space=pltpu.VMEM)] * 2,
        out_specs=pl.BlockSpec(memory_space=pltpu.HBM),
        scratch_shapes=[pltpu.VMEM(shape, jnp.float32), pltpu.SemaphoreType.DMA((qcount,))],
        compiler_params=pltpu.CompilerParams(vmem_limit_bytes=24 * 2**20),
        name="factors",
    )(parts, factors)


def local(tau_slabs, lambda_slabs, aux_factor, transfer_table):
    groups = lax.axis_size("kring")
    virtuals = tau_slabs.shape[2]
    contracted = tau_slabs.shape[3]
    qcount = aux_factor.shape[0]
    rows = tau_slabs.shape[0] * 2 * virtuals
    owned = virtuals // groups
    packed, slots = pack(
        tau_slabs.reshape(rows, contracted), lambda_slabs.reshape(rows, contracted), transfer_table
    )
    packed = packed.reshape(groups, contracted // groups, 2 * rows)
    start = groups - groups // 4
    ring = [group ^ 1 for group in [*range(start, groups), *range(start)]]
    exchanged = lax.all_to_all(packed, "kring", 0, 0, axis_index_groups=[ring])
    partial = pair_terms(slots, exchanged, virtuals, ring)
    near = ("kring", "y_lo", "z_lo")
    orb = ("y_lo", "z_hi", "z_lo")
    pieces = lax.axis_size(near) // groups
    members = [[group * pieces + piece for group in ring for piece in range(pieces)]]
    tiles = partial.reshape(lax.axis_size(near), SUBLANES, LANES).astype(jnp.float16)
    tiles = lax.all_to_all(tiles, near, 0, 0, axis_index_groups=members).astype(jnp.float32)
    exponents = tiles[:, owned : owned + 1, :]
    largest = exponents.max(0)
    tile = (tiles * jnp.exp2(exponents - HEADROOM)).sum(0) * jnp.exp2(SUM_HEADROOM - largest)
    tile = jnp.concatenate([tile[:owned], largest], 0).astype(jnp.float16)
    copies = jnp.broadcast_to(tile[None], (lax.axis_size(orb),) + tile.shape)
    depth = lax.axis_size(orb) // 2
    late = depth * 5 // 8
    order = [[*range(late, depth), *range(late), *range(depth, 2 * depth)]]
    parts = lax.all_to_all(copies, orb, 0, 0, axis_index_groups=order).astype(jnp.float32)
    factors = aux_factor.reshape(qcount, 2 * virtuals, aux_factor.shape[3])
    gamma = factor_product(parts, factors, owned, lax.axis_size("z_hi"))
    return gamma.transpose(0, 2, 1, 3)


def solution(mesh):
    groups, spread = mesh.devices.shape
    parts = jax.sharding.Mesh(
        mesh.devices.reshape(groups, 2, spread // 4, 2), ("kring", "y_lo", "z_hi", "z_lo")
    )
    orb = ("y_lo", "z_hi", "z_lo")
    in_specs = (
        P("kring", None, None, orb),
        P("kring", None, None, orb),
        P(None, None, None, orb),
        P(),
    )
    out_specs = P(None, None, "kring", orb)
    return jax.shard_map(local, mesh=parts, in_specs=in_specs, out_specs=out_specs, check_vma=False)
```

```python
import jax
import jax.numpy as jnp
from jax import lax
from jax.experimental import pallas as pl
from jax.experimental.pallas import tpu as pltpu
from jax.sharding import PartitionSpec as P

LANES = 128
SUBLANES = 8
SMALLEST = 2.0**-100
HEADROOM = 13.0
SUM_HEADROOM = 7.0


def partner_slots(table, shape):
    none = 2
    column = lax.broadcasted_iota(jnp.int32, table.shape, 1)
    used = table != none
    first = jnp.min(jnp.where(used, column, table.shape[1] - 1), 1, keepdims=True)
    last = jnp.max(jnp.where(used, column, 0), 1, keepdims=True)
    first_q = jnp.sum(jnp.where(column == first, table, 0), 1, keepdims=True)
    last_q = jnp.sum(jnp.where(column == last, table, 0), 1, keepdims=True)
    last_q = jnp.where(last == first, none, last_q)
    place = lax.broadcasted_iota(jnp.int32, shape, 1)
    return jnp.where(
        place == 0, first, jnp.where(place == 1, last, jnp.where(place == 2, first_q, last_q))
    )


def pack_kernel(
    tau_ref, lambda_ref, table_ref, packed_ref, slots_ref, both, table_here, arrived
):
    rows, contracted = tau_ref.shape
    tiles = contracted // LANES
    table_copy = pltpu.make_async_copy(table_ref, table_here, arrived.at[2 * tiles])
    table_copy.start()
    incoming = []
    for tile in range(tiles):
        lanes = pl.ds(tile * LANES, LANES)
        for part, source in enumerate((tau_ref, lambda_ref)):
            incoming.append(
                pltpu.make_async_copy(
                    source.at[:, lanes],
                    both.at[tile, pl.ds(part * rows, rows)],
                    arrived.at[2 * tile + part],
                )
            )
    for copy in incoming:
        copy.start()
    table_copy.wait()
    slots_ref[...] = partner_slots(table_here[...], slots_ref.shape)
    for tile in range(tiles):
        incoming[2 * tile].wait()
        incoming[2 * tile + 1].wait()
        packed_ref[tile * LANES : (tile + 1) * LANES] = both[tile].T


def pack(tau_rows, lambda_rows, table):
    rows, contracted = tau_rows.shape
    tiles = contracted // LANES
    return pl.pallas_call(
        pack_kernel,
        out_shape=(
            jax.ShapeDtypeStruct((contracted, 2 * rows), jnp.bfloat16),
            jax.ShapeDtypeStruct((table.shape[0], LANES), jnp.int32),
        ),
        in_specs=[pl.BlockSpec(memory_space=pltpu.HBM)] * 3,
        out_specs=(pl.BlockSpec(memory_space=pltpu.VMEM),) * 2,
        scratch_shapes=[
            pltpu.VMEM((tiles, 2 * rows, LANES), jnp.bfloat16),
            pltpu.VMEM(table.shape, jnp.int32),
            pltpu.SemaphoreType.DMA((2 * tiles + 1,)),
        ],
        compiler_params=pltpu.CompilerParams(vmem_limit_bytes=16 * 2**20),
        name="pack",
    )(*(pltpu.with_memory_space_constraint(x, pltpu.HBM) for x in (tau_rows, lambda_rows, table)))


def pair_kernel(
    virtuals, ring, slots_ref, packed_ref, out_ref, tau_part, lambda_part, chosen, slots, arrived
):
    slots_copy = pltpu.make_async_copy(slots_ref, slots, arrived)
    slots_copy.start()
    groups, depth, width = packed_ref.shape
    triples = 2 * groups
    slot_rows = tau_part.shape[1]
    qcount = 2
    half = width // 2
    fill = jnp.zeros((slot_rows - depth, half), jnp.float32)
    lane_fill = jnp.zeros((slot_rows, LANES - virtuals), jnp.bfloat16)
    for place, group in enumerate(ring):
        block = packed_ref[place].astype(jnp.float32)
        tau_block = jnp.concatenate([block[:, :half], fill], 0).astype(jnp.bfloat16)
        lambda_block = jnp.concatenate([block[:, half:], fill], 0).astype(jnp.bfloat16)
        for local_triple in range(2):
            start = local_triple * 2 * virtuals
            tau_part[2 * group + local_triple] = tau_block[:, start : start + 2 * virtuals]
            lambda_part[2 * group + local_triple] = jnp.concatenate(
                [
                    lambda_block[:, start : start + virtuals],
                    lane_fill,
                    lambda_block[:, start + virtuals : start + 2 * virtuals],
                    lane_fill,
                ],
                1,
            )

    slots_copy.wait()

    def choose(slot, triple):
        value = lambda_part[slots[triple, slot]]
        transfer = slots[triple, 2 + slot]
        for q in range(qcount):
            lane = (slot * qcount + q) * 2 * LANES
            chosen[triple, :, lane : lane + 2 * LANES] = jnp.where(
                transfer == q, value, jnp.zeros_like(value)
            )

    for triple in range(triples):
        choose(0, triple)
        choose(1, triple)
    tau_all = tau_part[...].reshape(triples * slot_rows, 2 * virtuals)
    wide = qcount * 2 * LANES
    products = lax.dot_general(
        tau_all,
        chosen[...].reshape(triples * slot_rows, 2 * wide),
        (((0,), (0,)), ((), ())),
        preferred_element_type=jnp.float32,
    )
    total = products[:, :wide] + products[:, wide:]
    owned = virtuals // groups
    pieces = []
    for q in range(qcount):
        lane = q * 2 * LANES
        real_lambda = total[:, lane : lane + LANES]
        imag_lambda = total[:, lane + LANES : lane + 2 * LANES]
        pieces.append(real_lambda[:virtuals] + imag_lambda[virtuals:])
        pieces.append(real_lambda[virtuals:] - imag_lambda[:virtuals])
    largest = jnp.abs(pieces[0])
    for piece in pieces[1:]:
        largest = jnp.maximum(largest, jnp.abs(piece))
    largest = jnp.max(jnp.max(largest, 0, keepdims=True), 1, keepdims=True)
    exponent = jnp.floor(jnp.log2(jnp.maximum(largest, SMALLEST)))
    scale = jnp.exp2(HEADROOM - exponent)
    note = jnp.broadcast_to(exponent, (SUBLANES - owned, LANES))
    for number, piece in enumerate(pieces):
        scaled = piece * scale
        for place, group in enumerate(ring):
            out_ref[place, number * SUBLANES : (number + 1) * SUBLANES] = jnp.concatenate(
                [scaled[group * owned : (group + 1) * owned], note], 0
            ).astype(out_ref.dtype)


def pair_terms(slots, packed, virtuals, ring):
    groups, depth, width = packed.shape
    slot_rows = -(-depth // 16) * 16
    triples = 2 * groups
    return pl.pallas_call(
        lambda *refs: pair_kernel(virtuals, ring, *refs),
        out_shape=jax.ShapeDtypeStruct((groups, 4 * SUBLANES, LANES), jnp.float32),
        in_specs=[pl.BlockSpec(memory_space=pl.ANY), pl.BlockSpec(memory_space=pltpu.VMEM)],
        out_specs=pl.BlockSpec(memory_space=pltpu.VMEM),
        scratch_shapes=[
            pltpu.VMEM((triples, slot_rows, 2 * virtuals), jnp.bfloat16),
            pltpu.VMEM((triples, slot_rows, 2 * LANES), jnp.bfloat16),
            pltpu.VMEM((triples, slot_rows, 8 * LANES), jnp.bfloat16),
            pltpu.SMEM(slots.shape, jnp.int32),
            pltpu.SemaphoreType.DMA,
        ],
        compiler_params=pltpu.CompilerParams(vmem_limit_bytes=40 * 2**20),
        name="pairs",
    )(slots, packed)


def factor_kernel(far, parts_ref, factors_ref, out_ref, held, left):
    qcount, depth, _ = factors_ref.shape
    owned = out_ref.shape[1]
    virtuals = depth // 2

    def unscaled(at, component):
        part = parts_ref[at, component * SUBLANES : (component + 1) * SUBLANES]
        return part * jnp.exp2(part[owned : owned + 1] - SUM_HEADROOM)

    outgoing = []
    for q in range(qcount):
        density = []
        for component in range(2):
            total = unscaled(q, component)
            for step in range(1, far):
                total += unscaled(step * qcount + q, component)
            density.append(total[:, :virtuals].astype(jnp.bfloat16).astype(jnp.float32))
        real, imag = density
        upper = jnp.concatenate([real, -imag], 1)
        lower = jnp.concatenate([imag, real], 1)
        rows = jnp.concatenate([upper, lower], 0).astype(jnp.bfloat16)
        gamma = jnp.dot(rows, factors_ref[q], preferred_element_type=jnp.float32)
        for row in range(owned):
            held[q, row] = jnp.concatenate(
                [gamma[row : row + 1], gamma[SUBLANES + row : SUBLANES + row + 1]], 0
            )
        copy = pltpu.make_async_copy(held.at[q], out_ref.at[q], left.at[q])
        copy.start()
        outgoing.append(copy)
    for copy in outgoing:
        copy.wait()


def factor_product(parts, factors, owned, far):
    qcount, _, columns = factors.shape
    shape = (qcount, owned, 2, columns)
    return pl.pallas_call(
        lambda *refs: factor_kernel(far, *refs),
        out_shape=jax.ShapeDtypeStruct(shape, jnp.float32),
        in_specs=[pl.BlockSpec(memory_space=pltpu.VMEM)] * 2,
        out_specs=pl.BlockSpec(memory_space=pltpu.HBM),
        scratch_shapes=[pltpu.VMEM(shape, jnp.float32), pltpu.SemaphoreType.DMA((qcount,))],
        compiler_params=pltpu.CompilerParams(vmem_limit_bytes=24 * 2**20),
        name="factors",
    )(parts, factors)


def local(tau_slabs, lambda_slabs, aux_factor, transfer_table):
    groups = lax.axis_size("kring")
    virtuals = tau_slabs.shape[2]
    contracted = tau_slabs.shape[3]
    qcount = aux_factor.shape[0]
    rows = tau_slabs.shape[0] * 2 * virtuals
    owned = virtuals // groups
    packed, slots = pack(
        tau_slabs.reshape(rows, contracted), lambda_slabs.reshape(rows, contracted), transfer_table
    )
    packed = packed.reshape(groups, contracted // groups, 2 * rows)
    start = groups - groups // 4
    ring = [group ^ 1 for group in [*range(start, groups), *range(start)]]
    exchanged = lax.all_to_all(packed, "kring", 0, 0, axis_index_groups=[ring])
    partial = pair_terms(slots, exchanged, virtuals, ring)
    near = ("kring", "y_lo", "z_lo")
    column = ("z_hi", "z_lo")
    pieces = lax.axis_size(near) // groups
    members = [[group * pieces + piece for group in ring for piece in range(pieces)]]
    height = 2 * SUBLANES
    tiles = partial.astype(jnp.float16).reshape(groups, 1, qcount, height, LANES)
    tiles = jnp.broadcast_to(tiles, (groups, pieces // qcount, qcount, height, LANES))
    tiles = tiles.reshape(groups * pieces, height, LANES)
    tiles = lax.all_to_all(tiles, near, 0, 0, axis_index_groups=members).astype(jnp.float32)
    exponents = tiles[:, owned : owned + 1, :]
    largest = exponents.max(0)
    tile = (tiles * jnp.exp2(exponents - HEADROOM)).sum(0) * jnp.exp2(SUM_HEADROOM - largest)
    second = SUBLANES + owned
    tile = jnp.concatenate([tile[:owned], largest, tile[SUBLANES:second], largest], 0)
    tile = tile.astype(jnp.float16)
    depth = lax.axis_size(column)
    copies = jnp.broadcast_to(tile[None], (depth,) + tile.shape)
    late = depth * 5 // 8
    order = [[*range(late, depth), *range(late)]]
    parts = lax.all_to_all(copies, column, 0, 0, axis_index_groups=order).astype(jnp.float32)
    factors = aux_factor.reshape(qcount, 2 * virtuals, aux_factor.shape[3])
    gamma = factor_product(parts, factors, owned, lax.axis_size("z_hi"))
    return gamma.transpose(0, 2, 1, 3)


def solution(mesh):
    groups, spread = mesh.devices.shape
    parts = jax.sharding.Mesh(
        mesh.devices.reshape(groups, 2, spread // 4, 2), ("kring", "y_lo", "z_hi", "z_lo")
    )
    orb = ("y_lo", "z_hi", "z_lo")
    in_specs = (
        P("kring", None, None, orb),
        P("kring", None, None, orb),
        P(None, None, None, orb),
        P(),
    )
    out_specs = P(None, None, "kring", orb)
    return jax.shard_map(local, mesh=parts, in_specs=in_specs, out_specs=out_specs, check_vma=False)
```

```python
import jax
import jax.numpy as jnp
from jax import lax
from jax.experimental import pallas as pl
from jax.experimental.pallas import tpu as pltpu
from jax.sharding import PartitionSpec as P

LANES = 128
SUBLANES = 8
SMALLEST = 2.0**-100
HEADROOM = 13.0
SUM_HEADROOM = 7.0


def partner_slots(table, shape):
    none = 2
    column = lax.broadcasted_iota(jnp.int32, table.shape, 1)
    used = table != none
    first = jnp.min(jnp.where(used, column, table.shape[1] - 1), 1, keepdims=True)
    last = jnp.max(jnp.where(used, column, 0), 1, keepdims=True)
    first_q = jnp.sum(jnp.where(column == first, table, 0), 1, keepdims=True)
    last_q = jnp.sum(jnp.where(column == last, table, 0), 1, keepdims=True)
    last_q = jnp.where(last == first, none, last_q)
    place = lax.broadcasted_iota(jnp.int32, shape, 1)
    return jnp.where(
        place == 0, first, jnp.where(place == 1, last, jnp.where(place == 2, first_q, last_q))
    )


def pack_kernel(
    tau_ref, lambda_ref, table_ref, packed_ref, slots_ref, both, table_here, arrived
):
    rows, contracted = tau_ref.shape
    tiles = contracted // LANES
    table_copy = pltpu.make_async_copy(table_ref, table_here, arrived.at[2 * tiles])
    table_copy.start()
    incoming = []
    for tile in range(tiles):
        lanes = pl.ds(tile * LANES, LANES)
        for part, source in enumerate((tau_ref, lambda_ref)):
            incoming.append(
                pltpu.make_async_copy(
                    source.at[:, lanes],
                    both.at[tile, pl.ds(part * rows, rows)],
                    arrived.at[2 * tile + part],
                )
            )
    for copy in incoming:
        copy.start()
    table_copy.wait()
    slots_ref[...] = partner_slots(table_here[...], slots_ref.shape)
    for tile in range(tiles):
        incoming[2 * tile].wait()
        incoming[2 * tile + 1].wait()
        packed_ref[tile * LANES : (tile + 1) * LANES] = both[tile].T


def pack(tau_rows, lambda_rows, table):
    rows, contracted = tau_rows.shape
    tiles = contracted // LANES
    return pl.pallas_call(
        pack_kernel,
        out_shape=(
            jax.ShapeDtypeStruct((contracted, 2 * rows), jnp.bfloat16),
            jax.ShapeDtypeStruct((table.shape[0], LANES), jnp.int32),
        ),
        in_specs=[pl.BlockSpec(memory_space=pltpu.HBM)] * 3,
        out_specs=(pl.BlockSpec(memory_space=pltpu.VMEM),) * 2,
        scratch_shapes=[
            pltpu.VMEM((tiles, 2 * rows, LANES), jnp.bfloat16),
            pltpu.VMEM(table.shape, jnp.int32),
            pltpu.SemaphoreType.DMA((2 * tiles + 1,)),
        ],
        compiler_params=pltpu.CompilerParams(vmem_limit_bytes=16 * 2**20),
        name="pack",
    )(*(pltpu.with_memory_space_constraint(x, pltpu.HBM) for x in (tau_rows, lambda_rows, table)))


def pair_kernel(
    virtuals, ring, slots_ref, packed_ref, out_ref, tau_part, lambda_part, chosen, slots, arrived
):
    slots_copy = pltpu.make_async_copy(slots_ref, slots, arrived)
    slots_copy.start()
    groups, depth, width = packed_ref.shape
    triples = 2 * groups
    slot_rows = tau_part.shape[1]
    qcount = 2
    half = width // 2
    fill = jnp.zeros((slot_rows - depth, half), jnp.float32)
    lane_fill = jnp.zeros((slot_rows, LANES - virtuals), jnp.bfloat16)
    for place, group in enumerate(ring):
        block = packed_ref[place].astype(jnp.float32)
        tau_block = jnp.concatenate([block[:, :half], fill], 0).astype(jnp.bfloat16)
        lambda_block = jnp.concatenate([block[:, half:], fill], 0).astype(jnp.bfloat16)
        for local_triple in range(2):
            start = local_triple * 2 * virtuals
            tau_part[2 * group + local_triple] = tau_block[:, start : start + 2 * virtuals]
            lambda_part[2 * group + local_triple] = jnp.concatenate(
                [
                    lambda_block[:, start : start + virtuals],
                    lane_fill,
                    lambda_block[:, start + virtuals : start + 2 * virtuals],
                    lane_fill,
                ],
                1,
            )

    slots_copy.wait()

    def choose(slot, triple):
        value = lambda_part[slots[triple, slot]]
        transfer = slots[triple, 2 + slot]
        for q in range(qcount):
            lane = (slot * qcount + q) * 2 * LANES
            chosen[triple, :, lane : lane + 2 * LANES] = jnp.where(
                transfer == q, value, jnp.zeros_like(value)
            )

    wide = qcount * 2 * LANES
    total = jnp.zeros((2 * virtuals, wide), jnp.float32)
    part = triples // 2
    for first in range(0, triples, part):
        for triple in range(first, first + part):
            choose(0, triple)
            choose(1, triple)
        products = lax.dot_general(
            tau_part[first : first + part].reshape(part * slot_rows, 2 * virtuals),
            chosen[first : first + part].reshape(part * slot_rows, 2 * wide),
            (((0,), (0,)), ((), ())),
            preferred_element_type=jnp.float32,
        )
        total += products[:, :wide] + products[:, wide:]
    owned = virtuals // groups
    pieces = []
    for q in range(qcount):
        lane = q * 2 * LANES
        real_lambda = total[:, lane : lane + LANES]
        imag_lambda = total[:, lane + LANES : lane + 2 * LANES]
        pieces.append(real_lambda[:virtuals] + imag_lambda[virtuals:])
        pieces.append(real_lambda[virtuals:] - imag_lambda[:virtuals])
    largest = jnp.abs(pieces[0])
    for piece in pieces[1:]:
        largest = jnp.maximum(largest, jnp.abs(piece))
    largest = jnp.max(jnp.max(largest, 0, keepdims=True), 1, keepdims=True)
    exponent = jnp.floor(jnp.log2(jnp.maximum(largest, SMALLEST)))
    scale = jnp.exp2(HEADROOM - exponent)
    note = jnp.broadcast_to(exponent, (SUBLANES - owned, LANES))
    for number, piece in enumerate(pieces):
        scaled = piece * scale
        for place, group in enumerate(ring):
            out_ref[place, number * SUBLANES : (number + 1) * SUBLANES] = jnp.concatenate(
                [scaled[group * owned : (group + 1) * owned], note], 0
            ).astype(out_ref.dtype)


def pair_terms(slots, packed, virtuals, ring):
    groups, depth, width = packed.shape
    slot_rows = -(-depth // 16) * 16
    triples = 2 * groups
    return pl.pallas_call(
        lambda *refs: pair_kernel(virtuals, ring, *refs),
        out_shape=jax.ShapeDtypeStruct((groups, 4 * SUBLANES, LANES), jnp.float32),
        in_specs=[pl.BlockSpec(memory_space=pl.ANY), pl.BlockSpec(memory_space=pltpu.VMEM)],
        out_specs=pl.BlockSpec(memory_space=pltpu.VMEM),
        scratch_shapes=[
            pltpu.VMEM((triples, slot_rows, 2 * virtuals), jnp.bfloat16),
            pltpu.VMEM((triples, slot_rows, 2 * LANES), jnp.bfloat16),
            pltpu.VMEM((triples, slot_rows, 8 * LANES), jnp.bfloat16),
            pltpu.SMEM(slots.shape, jnp.int32),
            pltpu.SemaphoreType.DMA,
        ],
        compiler_params=pltpu.CompilerParams(vmem_limit_bytes=40 * 2**20),
        name="pairs",
    )(slots, packed)


def factor_kernel(far, parts_ref, factors_ref, out_ref, held, left):
    qcount, depth, _ = factors_ref.shape
    owned = out_ref.shape[1]
    virtuals = depth // 2

    def unscaled(at):
        part = parts_ref[at]
        return part * jnp.exp2(part[owned : owned + 1] - SUM_HEADROOM)

    outgoing = []
    for q in range(qcount):
        density = []
        for component in range(2):
            total = unscaled(q * far * 2 + component)
            for step in range(1, far):
                total += unscaled((q * far + step) * 2 + component)
            density.append(total[:, :virtuals].astype(jnp.bfloat16).astype(jnp.float32))
        real, imag = density
        upper = jnp.concatenate([real, -imag], 1)
        lower = jnp.concatenate([imag, real], 1)
        rows = jnp.concatenate([upper, lower], 0).astype(jnp.bfloat16)
        gamma = jnp.dot(rows, factors_ref[q], preferred_element_type=jnp.float32)
        for row in range(owned):
            held[q, row] = jnp.concatenate(
                [gamma[row : row + 1], gamma[SUBLANES + row : SUBLANES + row + 1]], 0
            )
        copy = pltpu.make_async_copy(held.at[q], out_ref.at[q], left.at[q])
        copy.start()
        outgoing.append(copy)
    for copy in outgoing:
        copy.wait()


def factor_product(parts, factors, owned, far):
    qcount, _, columns = factors.shape
    shape = (qcount, owned, 2, columns)
    return pl.pallas_call(
        lambda *refs: factor_kernel(far, *refs),
        out_shape=jax.ShapeDtypeStruct(shape, jnp.float32),
        in_specs=[pl.BlockSpec(memory_space=pltpu.VMEM)] * 2,
        out_specs=pl.BlockSpec(memory_space=pltpu.HBM),
        scratch_shapes=[pltpu.VMEM(shape, jnp.float32), pltpu.SemaphoreType.DMA((qcount,))],
        compiler_params=pltpu.CompilerParams(vmem_limit_bytes=24 * 2**20),
        name="factors",
    )(parts, factors)


def local(tau_slabs, lambda_slabs, aux_factor, transfer_table):
    groups = lax.axis_size("kring")
    virtuals = tau_slabs.shape[2]
    contracted = tau_slabs.shape[3]
    qcount = aux_factor.shape[0]
    rows = tau_slabs.shape[0] * 2 * virtuals
    owned = virtuals // groups
    packed, slots = pack(
        tau_slabs.reshape(rows, contracted), lambda_slabs.reshape(rows, contracted), transfer_table
    )
    packed = packed.reshape(groups, contracted // groups, 2 * rows)
    start = groups - groups // 4
    ring = [group ^ 1 for group in [*range(start, groups), *range(start)]]
    exchanged = lax.all_to_all(packed, "kring", 0, 0, axis_index_groups=[ring])
    partial = pair_terms(slots, exchanged, virtuals, ring)
    near = ("kring", "y_lo", "z_lo")
    orb = ("y_lo", "z_hi", "z_lo")
    pieces = lax.axis_size(near) // groups
    members = [[group * pieces + piece for group in ring for piece in range(pieces)]]
    tiles = partial.reshape(lax.axis_size(near), SUBLANES, LANES).astype(jnp.float16)
    tiles = lax.all_to_all(tiles, near, 0, 0, axis_index_groups=members).astype(jnp.float32)
    exponents = tiles[:, owned : owned + 1, :]
    largest = exponents.max(0)
    tile = (tiles * jnp.exp2(exponents - HEADROOM)).sum(0) * jnp.exp2(SUM_HEADROOM - largest)
    tile = jnp.concatenate([tile[:owned], largest], 0).astype(jnp.float16)
    copies = jnp.broadcast_to(tile[None], (lax.axis_size(orb),) + tile.shape)
    depth = lax.axis_size(orb) // 2
    late = depth * 5 // 8
    order = [[*range(late, depth), *range(late), *range(depth, 2 * depth)]]
    parts = lax.all_to_all(copies, orb, 0, 0, axis_index_groups=order).astype(jnp.float32)
    factors = aux_factor.reshape(qcount, 2 * virtuals, aux_factor.shape[3])
    gamma = factor_product(parts, factors, owned, lax.axis_size("z_hi"))
    return gamma.transpose(0, 2, 1, 3)


def solution(mesh):
    groups, spread = mesh.devices.shape
    parts = jax.sharding.Mesh(
        mesh.devices.reshape(groups, 2, spread // 4, 2), ("kring", "y_lo", "z_hi", "z_lo")
    )
    orb = ("y_lo", "z_hi", "z_lo")
    in_specs = (
        P("kring", None, None, orb),
        P("kring", None, None, orb),
        P(None, None, None, orb),
        P(),
    )
    out_specs = P(None, None, "kring", orb)
    return jax.shard_map(local, mesh=parts, in_specs=in_specs, out_specs=out_specs, check_vma=False)
```

```python
import jax
import jax.numpy as jnp
from jax import lax
from jax.experimental import pallas as pl
from jax.experimental.pallas import tpu as pltpu
from jax.sharding import PartitionSpec as P

LANES = 128
SUBLANES = 8
SMALLEST = 2.0**-100
HEADROOM = 13.0
SUM_HEADROOM = 7.0


def partner_slots(table, shape):
    none = 2
    column = lax.broadcasted_iota(jnp.int32, table.shape, 1)
    used = table != none
    first = jnp.min(jnp.where(used, column, table.shape[1] - 1), 1, keepdims=True)
    last = jnp.max(jnp.where(used, column, 0), 1, keepdims=True)
    first_q = jnp.sum(jnp.where(column == first, table, 0), 1, keepdims=True)
    last_q = jnp.sum(jnp.where(column == last, table, 0), 1, keepdims=True)
    last_q = jnp.where(last == first, none, last_q)
    place = lax.broadcasted_iota(jnp.int32, shape, 1)
    return jnp.where(
        place == 0, first, jnp.where(place == 1, last, jnp.where(place == 2, first_q, last_q))
    )


def pack_kernel(
    tau_ref, lambda_ref, table_ref, packed_ref, slots_ref, both, table_here, arrived
):
    rows, contracted = tau_ref.shape
    tiles = contracted // LANES
    table_copy = pltpu.make_async_copy(table_ref, table_here, arrived.at[2 * tiles])
    table_copy.start()
    incoming = []
    for tile in range(tiles):
        lanes = pl.ds(tile * LANES, LANES)
        for part, source in enumerate((tau_ref, lambda_ref)):
            incoming.append(
                pltpu.make_async_copy(
                    source.at[:, lanes],
                    both.at[tile, pl.ds(part * rows, rows)],
                    arrived.at[2 * tile + part],
                )
            )
    for copy in incoming:
        copy.start()
    for tile in range(tiles):
        incoming[2 * tile].wait()
        incoming[2 * tile + 1].wait()
        packed_ref[tile * LANES : (tile + 1) * LANES] = both[tile].T
    table_copy.wait()
    slots_ref[...] = partner_slots(table_here[...], slots_ref.shape)


def pack(tau_rows, lambda_rows, table):
    rows, contracted = tau_rows.shape
    tiles = contracted // LANES
    return pl.pallas_call(
        pack_kernel,
        out_shape=(
            jax.ShapeDtypeStruct((contracted, 2 * rows), jnp.bfloat16),
            jax.ShapeDtypeStruct((table.shape[0], LANES), jnp.int32),
        ),
        in_specs=[pl.BlockSpec(memory_space=pltpu.HBM)] * 3,
        out_specs=(pl.BlockSpec(memory_space=pltpu.VMEM),) * 2,
        scratch_shapes=[
            pltpu.VMEM((tiles, 2 * rows, LANES), jnp.bfloat16),
            pltpu.VMEM(table.shape, jnp.int32),
            pltpu.SemaphoreType.DMA((2 * tiles + 1,)),
        ],
        compiler_params=pltpu.CompilerParams(vmem_limit_bytes=16 * 2**20),
        name="pack",
    )(*(pltpu.with_memory_space_constraint(x, pltpu.HBM) for x in (tau_rows, lambda_rows, table)))


def pair_kernel(
    virtuals, ring, slots_ref, packed_ref, out_ref, tau_part, lambda_part, chosen, slots, arrived
):
    slots_copy = pltpu.make_async_copy(slots_ref, slots, arrived)
    slots_copy.start()
    groups, depth, width = packed_ref.shape
    triples = 2 * groups
    slot_rows = tau_part.shape[1]
    qcount = 2
    half = width // 2
    fill = jnp.zeros((slot_rows - depth, half), jnp.float32)
    lane_fill = jnp.zeros((slot_rows, LANES - virtuals), jnp.bfloat16)
    for place, group in enumerate(ring):
        block = packed_ref[place].astype(jnp.float32)
        tau_block = jnp.concatenate([block[:, :half], fill], 0).astype(jnp.bfloat16)
        lambda_block = jnp.concatenate([block[:, half:], fill], 0).astype(jnp.bfloat16)
        for local_triple in range(2):
            start = local_triple * 2 * virtuals
            tau_part[2 * group + local_triple] = tau_block[:, start : start + 2 * virtuals]
            lambda_part[2 * group + local_triple] = jnp.concatenate(
                [
                    lambda_block[:, start : start + virtuals],
                    lane_fill,
                    lambda_block[:, start + virtuals : start + 2 * virtuals],
                    lane_fill,
                ],
                1,
            )

    slots_copy.wait()

    def choose(slot, triple):
        value = lambda_part[slots[triple, slot]]
        transfer = slots[triple, 2 + slot]
        for q in range(qcount):
            lane = (slot * qcount + q) * 2 * LANES
            chosen[triple, :, lane : lane + 2 * LANES] = jnp.where(
                transfer == q, value, jnp.zeros_like(value)
            )

    for triple in range(triples):
        choose(0, triple)
        choose(1, triple)
    tau_all = tau_part[...].reshape(triples * slot_rows, 2 * virtuals)
    wide = qcount * 2 * LANES
    products = lax.dot_general(
        tau_all,
        chosen[...].reshape(triples * slot_rows, 2 * wide),
        (((0,), (0,)), ((), ())),
        preferred_element_type=jnp.float32,
    )
    total = products[:, :wide] + products[:, wide:]
    owned = virtuals // groups
    pieces = []
    for q in range(qcount):
        lane = q * 2 * LANES
        real_lambda = total[:, lane : lane + LANES]
        imag_lambda = total[:, lane + LANES : lane + 2 * LANES]
        pieces.append(real_lambda[:virtuals] + imag_lambda[virtuals:])
        pieces.append(real_lambda[virtuals:] - imag_lambda[:virtuals])
    largest = jnp.abs(pieces[0])
    for piece in pieces[1:]:
        largest = jnp.maximum(largest, jnp.abs(piece))
    largest = jnp.max(jnp.max(largest, 0, keepdims=True), 1, keepdims=True)
    exponent = jnp.floor(jnp.log2(jnp.maximum(largest, SMALLEST)))
    scale = jnp.exp2(HEADROOM - exponent)
    note = jnp.broadcast_to(exponent, (SUBLANES - owned, LANES))
    for number, piece in enumerate(pieces):
        scaled = piece * scale
        for place, group in enumerate(ring):
            out_ref[place, number * SUBLANES : (number + 1) * SUBLANES] = jnp.concatenate(
                [scaled[group * owned : (group + 1) * owned], note], 0
            ).astype(out_ref.dtype)


def pair_terms(slots, packed, virtuals, ring):
    groups, depth, width = packed.shape
    slot_rows = -(-depth // 16) * 16
    triples = 2 * groups
    return pl.pallas_call(
        lambda *refs: pair_kernel(virtuals, ring, *refs),
        out_shape=jax.ShapeDtypeStruct((groups, 4 * SUBLANES, LANES), jnp.float32),
        in_specs=[pl.BlockSpec(memory_space=pl.ANY), pl.BlockSpec(memory_space=pltpu.VMEM)],
        out_specs=pl.BlockSpec(memory_space=pltpu.VMEM),
        scratch_shapes=[
            pltpu.VMEM((triples, slot_rows, 2 * virtuals), jnp.bfloat16),
            pltpu.VMEM((triples, slot_rows, 2 * LANES), jnp.bfloat16),
            pltpu.VMEM((triples, slot_rows, 8 * LANES), jnp.bfloat16),
            pltpu.SMEM(slots.shape, jnp.int32),
            pltpu.SemaphoreType.DMA,
        ],
        compiler_params=pltpu.CompilerParams(vmem_limit_bytes=40 * 2**20),
        name="pairs",
    )(slots, packed)


def factor_kernel(far, parts_ref, factors_ref, out_ref, held, left):
    qcount, depth, _ = factors_ref.shape
    owned = out_ref.shape[1]
    virtuals = depth // 2

    def unscaled(at):
        part = parts_ref[at]
        return part * jnp.exp2(part[owned : owned + 1] - SUM_HEADROOM)

    outgoing = []
    for q in range(qcount):
        density = []
        for component in range(2):
            total = unscaled(q * far * 2 + component)
            for step in range(1, far):
                total += unscaled((q * far + step) * 2 + component)
            density.append(total[:, :virtuals].astype(jnp.bfloat16).astype(jnp.float32))
        real, imag = density
        upper = jnp.concatenate([real, -imag], 1)
        lower = jnp.concatenate([imag, real], 1)
        rows = jnp.concatenate([upper, lower], 0).astype(jnp.bfloat16)
        gamma = jnp.dot(rows, factors_ref[q], preferred_element_type=jnp.float32)
        for row in range(owned):
            held[q, row] = jnp.concatenate(
                [gamma[row : row + 1], gamma[SUBLANES + row : SUBLANES + row + 1]], 0
            )
        copy = pltpu.make_async_copy(held.at[q], out_ref.at[q], left.at[q])
        copy.start()
        outgoing.append(copy)
    for copy in outgoing:
        copy.wait()


def factor_product(parts, factors, owned, far):
    qcount, _, columns = factors.shape
    shape = (qcount, owned, 2, columns)
    return pl.pallas_call(
        lambda *refs: factor_kernel(far, *refs),
        out_shape=jax.ShapeDtypeStruct(shape, jnp.float32),
        in_specs=[pl.BlockSpec(memory_space=pltpu.VMEM)] * 2,
        out_specs=pl.BlockSpec(memory_space=pltpu.HBM),
        scratch_shapes=[pltpu.VMEM(shape, jnp.float32), pltpu.SemaphoreType.DMA((qcount,))],
        compiler_params=pltpu.CompilerParams(vmem_limit_bytes=24 * 2**20),
        name="factors",
    )(parts, factors)


def local(tau_slabs, lambda_slabs, aux_factor, transfer_table):
    groups = lax.axis_size("kring")
    virtuals = tau_slabs.shape[2]
    contracted = tau_slabs.shape[3]
    qcount = aux_factor.shape[0]
    rows = tau_slabs.shape[0] * 2 * virtuals
    owned = virtuals // groups
    packed, slots = pack(
        tau_slabs.reshape(rows, contracted), lambda_slabs.reshape(rows, contracted), transfer_table
    )
    packed = packed.reshape(groups, contracted // groups, 2 * rows)
    start = groups - groups // 4
    ring = [group ^ 1 for group in [*range(start, groups), *range(start)]]
    exchanged = lax.all_to_all(packed, "kring", 0, 0, axis_index_groups=[ring])
    partial = pair_terms(slots, exchanged, virtuals, ring)
    near = ("kring", "y_lo", "z_lo")
    orb = ("y_lo", "z_hi", "z_lo")
    pieces = lax.axis_size(near) // groups
    members = [[group * pieces + piece for group in ring for piece in range(pieces)]]
    tiles = partial.reshape(lax.axis_size(near), SUBLANES, LANES).astype(jnp.float16)
    tiles = lax.all_to_all(tiles, near, 0, 0, axis_index_groups=members).astype(jnp.float32)
    exponents = tiles[:, owned : owned + 1, :]
    largest = exponents.max(0)
    tile = (tiles * jnp.exp2(exponents - HEADROOM)).sum(0) * jnp.exp2(SUM_HEADROOM - largest)
    tile = jnp.concatenate([tile[:owned], largest], 0).astype(jnp.float16)
    copies = jnp.broadcast_to(tile[None], (lax.axis_size(orb),) + tile.shape)
    depth = lax.axis_size(orb) // 2
    late = depth * 5 // 8
    order = [[*range(late, depth), *range(late), *range(depth, 2 * depth)]]
    parts = lax.all_to_all(copies, orb, 0, 0, axis_index_groups=order).astype(jnp.float32)
    factors = aux_factor.reshape(qcount, 2 * virtuals, aux_factor.shape[3])
    gamma = factor_product(parts, factors, owned, lax.axis_size("z_hi"))
    return gamma.transpose(0, 2, 1, 3)


def solution(mesh):
    groups, spread = mesh.devices.shape
    parts = jax.sharding.Mesh(
        mesh.devices.reshape(groups, 2, spread // 4, 2), ("kring", "y_lo", "z_hi", "z_lo")
    )
    orb = ("y_lo", "z_hi", "z_lo")
    in_specs = (
        P("kring", None, None, orb),
        P("kring", None, None, orb),
        P(None, None, None, orb),
        P(),
    )
    out_specs = P(None, None, "kring", orb)
    return jax.shard_map(local, mesh=parts, in_specs=in_specs, out_specs=out_specs, check_vma=False)
```
